256 devices in a mesh: grp: 4 (over x_lo, core), pts: 64 (over y, x_hi, z).
Axes of the slice: x: 4 (x_hi: 2, x_lo: 2; x = x_hi * 2 + x_lo), y: 4, z: 8, core: 2. Of those that a mesh axis runs over, the one named last changes fastest.
Arguments:
- points: float32 [65536, 2048], P(('grp', 'pts')), may hold values from -2 to 2
- log_factor: float32 [65536, 256], P(('grp', 'pts')), may hold values from -40 to 320
- masses: float32 [65536], P(('grp', 'pts')), may hold values from 0.1 to 12
Outputs:
- factors: float32 [65536, 256], P(('grp', 'pts'))
The draws below stay inside these ranges and needn't reach their ends.
All inputs are finite; a program needn't handle non-finite values. Where the reference program divides by a largest or mean magnitude, that divisor is 1e-20 or more.
Results may differ from the reference program's by a relative error of at most 0.0003.
Values sent between devices are 32-bit elements; how exact they have to be, the bound alone decides.
A program may use at most 64 MiB of HBM per device.

```python
import math
import jax
import jax.numpy as jnp
from jax import lax

D = 2048
RANK = 256
ITERS = 2
ALL = 65536
NS = 49152
NT = 16384


def shared_latent(key):
    latent_width = 2 * RANK
    latent = jax.random.normal(jax.random.fold_in(key, 701), (ALL, latent_width), jnp.float32)
    anchors = jax.random.normal(jax.random.fold_in(key, 702), (RANK, latent_width), jnp.float32)
    return (latent, anchors)


def draw_points(key, part):
    latent, anchors = shared_latent(key)
    latent_width = latent.shape[1]
    latent_basis = jax.random.normal(jax.random.fold_in(key, 703), (latent_width, D), jnp.float32) / math.sqrt(D)
    shaped = jnp.dot(latent, latent_basis) / math.sqrt(latent_width)
    noise_part = jax.random.normal(jax.random.fold_in(key, 704), (ALL, D), jnp.float32)
    scales = jnp.exp(jax.random.uniform(jax.random.fold_in(key, 705), (ALL, 1), jnp.float32, math.log(0.4), math.log(4.0)))
    values = shaped + 0.5 * noise_part / math.sqrt(D)
    return jnp.clip(scales * values, -2.0, 2.0)


def draw_log_factor(key, part):
    latent, anchors = shared_latent(key)
    latent_width = latent.shape[1]
    aligned = 2.0 * jnp.dot(latent, anchors.T) / math.sqrt(latent_width)
    rough_part = jax.random.normal(jax.random.fold_in(key, 711), (ALL, RANK), jnp.float32)
    values = aligned + rough_part
    return jnp.clip(values, -40.0, 320.0)


def draw_masses(key, part):
    position = jnp.arange(ALL).astype(jnp.float32)
    within = jnp.where(position < NS, position / NS, (position - NS) / NT)
    lower_end = math.log(0.5)
    upper_end = math.log(2.0)
    rough_factor = jnp.exp(jax.random.uniform(jax.random.fold_in(key, 721), (ALL,), jnp.float32, lower_end, upper_end))
    return (1.0 + 2.0 * within) * rough_factor


def setup_inputs(seed: int = 0) -> dict:
    splits = jax.random.split(jax.random.key(seed), 4)
    points = draw_points(jax.random.fold_in(splits[3], 71), 0)
    log_factor = draw_log_factor(jax.random.fold_in(splits[3], 71), 0)
    masses = draw_masses(jax.random.fold_in(splits[3], 71), 0)
    return {"points": points, "log_factor": log_factor, "masses": masses}


step_scale = 4.0
highest = lax.Precision.HIGHEST


def side_sums(side_points, side_scaled):
    column_sums = jnp.sum(side_scaled, axis=0)
    mass_total = jnp.sum(column_sums)
    moment = lax.dot_general(side_points, side_scaled, (((0,), (0,)), ((), ())), precision=highest, preferred_element_type=jnp.float32) / mass_total
    squares = jnp.sum(side_points * side_points, axis=1)
    norm_moment = jnp.dot(squares, side_scaled, precision=highest, preferred_element_type=jnp.float32) / mass_total
    return column_sums / mass_total, moment, norm_moment


def cost_gradient(side_points, column_share, moment, norm_moment, marginal):
    squares = jnp.sum(side_points * side_points, axis=1)
    cross_term = jnp.dot(side_points, moment, precision=highest, preferred_element_type=jnp.float32)
    return (squares[:, None] * column_share[None, :] - 2.0 * cross_term + norm_moment[None, :]) / marginal[None, :]


def reference(points, log_factor, masses):
    source_points = points[:NS]
    target_points = points[NS:]
    for iteration in range(ITERS):
        weights = jax.nn.softmax(log_factor, axis=1)
        scaled = weights * masses[:, None]
        source_share, source_moment, source_norms = side_sums(source_points, scaled[:NS])
        target_share, target_moment, target_norms = side_sums(target_points, scaled[NS:])
        marginal = 0.5 * (source_share + target_share)
        source_gradient = cost_gradient(source_points, target_share, target_moment, target_norms, marginal)
        target_gradient = cost_gradient(target_points, source_share, source_moment, source_norms, marginal)
        gradient = jnp.concatenate([source_gradient, target_gradient], axis=0)
        centred = gradient - jnp.mean(gradient, axis=1, keepdims=True)
        step_rate = step_scale / (jnp.max(jnp.abs(centred)) + 1e-6)
        log_factor = log_factor - step_rate * gradient
    return RANK * jax.nn.softmax(log_factor, axis=1)
```

```python
import functools

import jax
import jax.numpy as jnp
from jax import lax
from jax.experimental import pallas as pl
from jax.experimental.pallas import tpu as pltpu
from jax.sharding import Mesh
from jax.sharding import PartitionSpec as P

ITERS = 2
STEP_SCALE = 4.0
AXES = ("xl", "c", "y", "xh", "z")
NY, NZ, NX = 4, 8, 4
ROWS = 256
RANK = 256
HALF = 1024
YB = HALF // NY
ZB = YB // NZ
ZS = ZB + 8
HIGHEST = lax.Precision.HIGHEST


def dot0(a, b):
    return lax.dot_general(
        a, b, (((0,), (0,)), ((), ())), precision=HIGHEST, preferred_element_type=jnp.float32
    )


def dot1(a, b):
    return lax.dot_general(
        a, b, (((1,), (0,)), ((), ())), precision=HIGHEST, preferred_element_type=jnp.float32
    )


def kernel(
    points, lf_in, mass, out,
    pts, lf, meta, meta_out, scaled, mom, ring1, ring2, stat, zsend, zrecv, xall, gath, acc, part,
    mx, grad, fin,
    s_pts, r_pts, s_lf, r_lf, s_meta, r_meta, s_sc, r_sc, s_r1, r_r1, s_r2, r_r2, s_st, r_st,
    s_z, r_z, s_x, r_x, s_gz, r_gz, s_gy, r_gy, s_pt, r_pt, s_mc, r_mc, s_my, r_my, s_mz, r_mz,
    s_fin, r_fin,
):
    xl, c, y, xh, z = (lax.axis_index(a) for a in AXES)
    x = 2 * xh + xl
    other = 1 - c
    swp = xl * ((c + xh) % 2)
    vc = (c + swp) % 2
    vxh = (xh + swp) % 2
    swapped = swp == 1

    def at(c_=None, x_=None, y_=None, z_=None):
        x_ = x if x_ is None else x_
        return (
            x_ % 2,
            c if c_ is None else c_,
            y if y_ is None else y_,
            x_ // 2,
            z if z_ is None else z_,
        )

    xq = 2 * vxh + xl
    yo = [(y + j) % NY for j in range(NY)]
    zo = [(z + j) % NZ for j in range(NZ)]
    xo = [(x + j) % NX for j in range(NX)]
    cx = [(c if i == 0 else other, xo[j]) for i in range(2) for j in range(NX)]

    def rdma(src, dst, ss, rs, dev):
        return pltpu.make_async_remote_copy(
            src_ref=src, dst_ref=dst, send_sem=ss, recv_sem=rs, device_id=dev,
            device_id_type=pl.DeviceIdType.MESH,
        )

    barrier = pltpu.get_barrier_semaphore()
    peers = [at(c_=a, x_=b) for a, b in cx[1:]]
    peers += [at(y_=b) for b in yo[1:]] + [at(z_=b) for b in zo[1:]]
    for p in peers:
        pl.semaphore_signal(barrier, inc=1, device_id=p, device_id_type=pl.DeviceIdType.MESH)
    pl.semaphore_wait(barrier, len(peers))

    def cols(h, b):
        return points.at[:, pl.ds(pl.multiple_of(h * HALF + b * YB, YB), YB)]

    order = [yo[2], yo[1], yo[3], yo[0]]
    mine = pl.ds(pl.multiple_of(vc * ROWS, ROWS), ROWS)

    def half_out(b):
        return rdma(cols(other, b), pts.at[b, mine], s_pts.at[0, b], r_pts.at[b, vc],
                    at(c_=other, x_=xq))

    def half_own(b):
        return rdma(cols(c, b), pts.at[b, mine], s_pts.at[1, b], r_pts.at[b, vc],
                    at(c_=c, x_=xq))

    def half_local(b):
        return pltpu.make_async_copy(cols(c, b), pts.at[b, mine], r_pts.at[b, vc])

    lf_remote = rdma(lf_in, lf, s_lf, r_lf, at(c_=vc, x_=xq))
    lf_local = pltpu.make_async_copy(lf_in, lf, r_lf)

    @pl.when(swapped)
    def _():
        lf_remote.start()
        for b in order:
            half_out(b).start()
            half_own(b).start()

    @pl.when(jnp.logical_not(swapped))
    def _():
        lf_local.start()
        for b in order:
            half_out(b).start()
            half_local(b).start()

    squares = jnp.zeros((ROWS, 1), jnp.float32)
    for k in range(8):
        part_k = points[:, k * 256 : (k + 1) * 256]
        squares += jnp.sum(part_k * part_k, axis=1, keepdims=True)
    lane = lax.broadcasted_iota(jnp.int32, (ROWS, 128), 1)
    meta_out[...] = jnp.where(
        lane == 0, squares, jnp.where(lane == 1, 1.0, jnp.where(lane == 2, mass[...], 0.0))
    )
    meta_remote = rdma(meta_out, meta.at[mine], s_meta.at[0], r_meta.at[vc],
                       at(c_=other, x_=xq))
    meta_own = rdma(meta_out, meta.at[mine], s_meta.at[1], r_meta.at[vc], at(c_=c, x_=xq))
    meta_local = pltpu.make_async_copy(meta_out, meta.at[mine], r_meta.at[vc])
    meta_remote.start()

    @pl.when(swapped)
    def _():
        meta_own.start()

    @pl.when(jnp.logical_not(swapped))
    def _():
        meta_local.start()

    own = pl.ds(pl.multiple_of(c * ROWS, ROWS), ROWS)
    oth = pl.ds(pl.multiple_of(other * ROWS, ROWS), ROWS)
    lf_remote.wait_recv()
    for v in range(2):
        rdma(meta_out, meta.at[pl.ds(v * ROWS, ROWS)], s_meta.at[0], r_meta.at[v],
             at(c_=other)).wait_recv()

    def wait_points(b):
        for v in range(2):
            rdma(cols(c, b), pts.at[b, pl.ds(v * ROWS, ROWS)], s_pts.at[0, b], r_pts.at[b, v],
                 at(c_=other)).wait_recv()

    def step(it, _):
        v = lf[...]
        e = jnp.exp(v - jnp.max(v, axis=1, keepdims=True))
        mass_own = meta[own, 2:3]
        scaled[it, own] = e / jnp.sum(e, axis=1, keepdims=True) * mass_own
        cp = rdma(scaled.at[it, own], scaled.at[it, own], s_sc.at[it], r_sc.at[it], at(c_=other))
        cp.start()
        cp.wait_send()
        rdma(scaled.at[it, oth], scaled.at[it, oth], s_sc.at[it], r_sc.at[it],
             at(c_=other)).wait_recv()

        stat[it, 0] = dot0(meta[...], scaled[it])[:8]
        st = [rdma(stat.at[it, 0], stat.at[it, j], s_st.at[it, j], r_st.at[it, j], at(y_=yo[j]))
              for j in range(1, NY)]
        for cpy in st:
            cpy.start()

        def moment(b):
            @pl.when(it == 0)
            def _():
                wait_points(b)
            return dot0(pts[b], scaled[it])

        mom[it, 2] = moment(yo[2])
        up1 = rdma(mom.at[it, 2, pl.ds(0, 128)], ring1.at[it, 0], s_r1.at[it, 0],
                   r_r1.at[it, 0], at(y_=yo[1]))
        dn1 = rdma(mom.at[it, 2, pl.ds(128, 128)], ring1.at[it, 1], s_r1.at[it, 1],
                   r_r1.at[it, 1], at(y_=yo[3]))
        up1.start()
        dn1.start()
        m1 = moment(yo[1])
        up1.wait_recv()
        mom[it, 1, :128] = m1[:128] + ring1[it, 0]
        mom[it, 1, 128:] = m1[128:]
        up2 = rdma(mom.at[it, 1], ring2.at[it, 0], s_r2.at[it, 0], r_r2.at[it, 0], at(y_=yo[1]))
        up2.start()
        m3 = moment(yo[3])
        dn1.wait_recv()
        mom[it, 3, :128] = m3[:128]
        mom[it, 3, 128:] = m3[128:] + ring1[it, 1]
        dn2 = rdma(mom.at[it, 3], ring2.at[it, 1], s_r2.at[it, 1], r_r2.at[it, 1], at(y_=yo[3]))
        dn2.start()
        mom[it, 0] = moment(yo[0])
        for cpy in st:
            cpy.wait_recv()
        stats_y = stat[it, 0] + stat[it, 1] + stat[it, 2] + stat[it, 3]
        for k in range(NZ):
            zsend[it, k, ZB:] = stats_y
        up2.wait_recv()
        dn2.wait_recv()
        for k in range(NZ):
            r = slice(k * ZB, (k + 1) * ZB)
            zsend[it, k, :ZB] = mom[it, 0, r] + ring2[it, 0, r] + ring2[it, 1, r]

        zc = [rdma(zsend.at[it, zo[j]], zrecv.at[it, j], s_z.at[it, j], r_z.at[it, j],
                   at(z_=zo[j])) for j in range(1, NZ)]
        for cpy in zc:
            cpy.start()
        shard = zsend[it, z]
        for j in range(1, NZ):
            zc[j - 1].wait_recv()
            shard += zrecv[it, j]

        xall[it, x] = shard
        xc = [rdma(xall.at[it, x], xall.at[it, x], s_x.at[it, j], r_x.at[it, j], at(x_=xo[j]))
              for j in range(1, NX)]
        for cpy in xc:
            cpy.start()
        for j in range(1, NX):
            xm = (x + NX - j) % NX
            rdma(xall.at[it, xm], xall.at[it, xm], s_x.at[it, j], r_x.at[it, j],
                 at(x_=xo[j])).wait_recv()
        source = xall[it, 0] + xall[it, 1] + xall[it, 2]
        target = xall[it, 3]
        is_target = x == 3
        facing = jnp.where(is_target, source, target)

        zrows = pl.ds(pl.multiple_of(z * ZB, ZB), ZB)
        gath[it, y, zrows] = facing[:ZB]
        gz = [rdma(gath.at[it, y, zrows], gath.at[it, y, zrows], s_gz.at[it, j], r_gz.at[it, j],
                   at(z_=zo[j])) for j in range(1, NZ)]
        for cpy in gz:
            cpy.start()
        source_mass = jnp.sum(source[ZB + 1 : ZB + 2])
        target_mass = jnp.sum(target[ZB + 1 : ZB + 2])
        facing_mass = jnp.where(is_target, source_mass, target_mass)
        marginal = 0.5 * (source[ZB + 1 : ZB + 2] / source_mass
                          + target[ZB + 1 : ZB + 2] / target_mass)
        for j in range(1, NZ):
            zr = pl.ds(pl.multiple_of(((z + NZ - j) % NZ) * ZB, ZB), ZB)
            rdma(gath.at[it, y, zr], gath.at[it, y, zr], s_gz.at[it, j], r_gz.at[it, j],
                 at(z_=zo[j])).wait_recv()
        gu1 = rdma(gath.at[it, y], gath.at[it, y], s_gy.at[it, 0], r_gy.at[it, 0], at(y_=yo[1]))
        gd1 = rdma(gath.at[it, y], gath.at[it, y], s_gy.at[it, 1], r_gy.at[it, 1], at(y_=yo[3]))
        gu1.start()
        gd1.start()
        acc[...] = dot1(pts[y], gath[it, y])

        def got(b, rows, k):
            r = gath.at[it, b, rows]
            rdma(r, r, s_gy.at[it, k], r_gy.at[it, k], at(y_=yo[1])).wait_recv()

        whole, lo, hi = pl.ds(0, YB), pl.ds(0, 128), pl.ds(128, 128)
        got(yo[3], whole, 0)
        gu2 = rdma(gath.at[it, yo[3], lo], gath.at[it, yo[3], lo], s_gy.at[it, 2],
                   r_gy.at[it, 2], at(y_=yo[1]))
        gu2.start()
        got(yo[1], whole, 1)
        gd2 = rdma(gath.at[it, yo[1], hi], gath.at[it, yo[1], hi], s_gy.at[it, 3],
                   r_gy.at[it, 3], at(y_=yo[3]))
        gd2.start()
        acc[...] += dot1(pts[yo[3]], gath[it, yo[3]])
        acc[...] += dot1(pts[yo[1]], gath[it, yo[1]])
        got(yo[2], lo, 2)
        got(yo[2], hi, 3)
        part[it, 0] = acc[oth] + dot1(pts[yo[2], oth], gath[it, yo[2]])
        pc = rdma(part.at[it, 0], part.at[it, 1], s_pt.at[it], r_pt.at[it], at(c_=other))
        pc.start()
        cross = acc[own] + dot1(pts[yo[2], own], gath[it, yo[2]])
        pc.wait_recv()
        cross += part[it, 1]

        facing_columns = facing[ZB + 1 : ZB + 2]
        facing_norms = facing[ZB : ZB + 1]
        squares_own = meta[own, 0:1]
        g = (
            squares_own * (facing_columns / facing_mass)
            - 2.0 * (cross / facing_mass)
            + facing_norms / facing_mass
        ) / marginal
        grad[...] = g
        centred = g - jnp.sum(g, axis=1, keepdims=True) * (1.0 / RANK)
        largest = jnp.max(jnp.abs(centred))

        last = it == ITERS - 1

        @pl.when(last)
        def _():
            @pl.when(swapped)
            def _():
                rdma(lf, fin.at[0], s_fin.at[0], r_fin.at[0], at(c_=vc, x_=xq)).start()
                rdma(grad, fin.at[1], s_fin.at[1], r_fin.at[1], at(c_=vc, x_=xq)).start()

        tile = (8, 128)
        mx[it, 0] = jnp.full(tile, largest)
        mc = [rdma(mx.at[it, 0], mx.at[it, j], s_mc.at[it, j], r_mc.at[it, j],
                   at(c_=cx[j][0], x_=cx[j][1])) for j in range(1, 8)]
        for cpy in mc:
            cpy.start()
        m = mx[it, 0]
        for j in range(1, 8):
            mc[j - 1].wait_recv()
        for j in range(1, 8):
            m = jnp.maximum(m, mx[it, j])
        mx[it, 8] = m
        my = [rdma(mx.at[it, 8], mx.at[it, 8 + j], s_my.at[it, j], r_my.at[it, j], at(y_=yo[j]))
              for j in range(1, NY)]
        for cpy in my:
            cpy.start()
        for cpy in my:
            cpy.wait_recv()
        for j in range(1, NY):
            m = jnp.maximum(m, mx[it, 8 + j])
        mx[it, 12] = m
        mz = [rdma(mx.at[it, 12], mx.at[it, 12 + j], s_mz.at[it, j], r_mz.at[it, j],
                   at(z_=zo[j])) for j in range(1, NZ)]
        for cpy in mz:
            cpy.start()
        for cpy in mz:
            cpy.wait_recv()
        for j in range(1, NZ):
            m = jnp.maximum(m, mx[it, 12 + j])
        rate = STEP_SCALE / (m[0:1, 0:1] + 1e-6)

        @pl.when(jnp.logical_not(last))
        def _():
            lf[...] = lf[...] - rate * grad[...]

        @pl.when(last)
        def _():
            def finish(a, b):
                u = a - rate * b
                ex = jnp.exp(u - jnp.max(u, axis=1, keepdims=True))
                out[...] = RANK * (ex / jnp.sum(ex, axis=1, keepdims=True))

            @pl.when(swapped)
            def _():
                for k, src in ((0, lf), (1, grad)):
                    cpy = rdma(src, fin.at[k], s_fin.at[k], r_fin.at[k], at(c_=vc, x_=xq))
                    cpy.wait_send()
                    cpy.wait_recv()
                finish(fin[0], fin[1])

            @pl.when(jnp.logical_not(swapped))
            def _():
                finish(lf[...], grad[...])

        for cpy in [up1, dn1, up2, dn2, gu1, gd1, gu2, gd2, pc] + st + zc + xc + gz + mc + my + mz:
            cpy.wait_send()
        return 0

    lax.fori_loop(0, ITERS, step, 0)

    for b in order:
        half_out(b).wait_send()
    meta_remote.wait_send()

    @pl.when(swapped)
    def _():
        for b in order:
            half_own(b).wait_send()
        lf_remote.wait_send()
        meta_own.wait_send()


def body(points, log_factor, masses):
    mass = jnp.broadcast_to(masses[:, None], (ROWS, 128))
    f32 = jnp.float32
    vm = lambda *s: pltpu.VMEM(s, f32)
    dma = lambda *s: pltpu.SemaphoreType.DMA(s)
    n = ITERS
    return pl.pallas_call(
        kernel,
        out_shape=jax.ShapeDtypeStruct((ROWS, RANK), f32),
        in_specs=[pl.BlockSpec(memory_space=pltpu.VMEM)] * 3,
        out_specs=pl.BlockSpec(memory_space=pltpu.VMEM),
        scratch_shapes=[
            vm(NY, 2 * ROWS, YB), vm(ROWS, RANK), vm(2 * ROWS, 128), vm(ROWS, 128),
            vm(n, 2 * ROWS, RANK), vm(n, NY, YB, RANK), vm(n, 2, 128, RANK), vm(n, 2, YB, RANK),
            vm(n, NY, 8, RANK), vm(n, NZ, ZS, RANK), vm(n, NZ, ZS, RANK), vm(n, NX, ZS, RANK),
            vm(n, NY, YB, RANK), vm(2 * ROWS, RANK), vm(n, 2, ROWS, RANK),
            vm(n, 20, 8, 128), vm(ROWS, RANK), vm(2, ROWS, RANK),
            dma(2, NY), dma(NY, 2), pltpu.SemaphoreType.DMA, pltpu.SemaphoreType.DMA,
            dma(2), dma(2), dma(n), dma(n), dma(n, 2), dma(n, 2), dma(n, 2), dma(n, 2),
            dma(n, NY), dma(n, NY), dma(n, NZ), dma(n, NZ), dma(n, NX), dma(n, NX),
            dma(n, NZ), dma(n, NZ), dma(n, 4), dma(n, 4), dma(n), dma(n),
            dma(n, 8), dma(n, 8), dma(n, NY), dma(n, NY), dma(n, NZ), dma(n, NZ),
            dma(2), dma(2),
        ],
        compiler_params=pltpu.CompilerParams(
            collective_id=0, has_side_effects=True, vmem_limit_bytes=48 << 20
        ),
        name="steps",
    )(points, log_factor, mass)


def solution(mesh):
    split = Mesh(mesh.devices.reshape(2, 2, 4, 2, 8), AXES)
    rows = ("xl", "c", "y", "xh", "z")
    return jax.shard_map(
        body,
        mesh=split,
        in_specs=(P(rows, None), P(rows, None), P(rows)),
        out_specs=P(rows, None),
        check_vma=False,
    )
```

```python
import functools

import jax
import jax.numpy as jnp
from jax import lax
from jax.experimental import pallas as pl
from jax.experimental.pallas import tpu as pltpu
from jax.sharding import Mesh
from jax.sharding import PartitionSpec as P

ITERS = 2
STEP_SCALE = 4.0
AXES = ("xl", "c", "y", "xh", "z")
NY, NZ, NX = 4, 8, 4
ROWS = 256
RANK = 256
HALF = 1024
YB = HALF // NY
ZB = YB // NZ
ZS = ZB + 8
HIGHEST = lax.Precision.HIGHEST


def dot0(a, b):
    return lax.dot_general(
        a, b, (((0,), (0,)), ((), ())), precision=HIGHEST, preferred_element_type=jnp.float32
    )


def dot1(a, b):
    return lax.dot_general(
        a, b, (((1,), (0,)), ((), ())), precision=HIGHEST, preferred_element_type=jnp.float32
    )


def kernel(
    points, lf_in, mass, out,
    pts, pv, relay, lf, meta, meta_out, percol, scaled, mom, ring1, ring2, stat, zsend, zrecv, xall, gath, acc, part,
    mx, grad, fin,
    r_pv, s_rel, r_rel, s_fwd, s_pts, r_pts, s_lf, r_lf, s_meta, r_meta, s_sc, r_sc, s_r1, r_r1, s_r2, r_r2, s_st, r_st,
    s_z, r_z, s_x, r_x, s_gz, r_gz, s_gy, r_gy, s_pt, r_pt, s_mc, r_mc, s_my, r_my,
    s_fin, r_fin,
):
    xl, c, y, xh, z = (lax.axis_index(a) for a in AXES)
    x = 2 * xh + xl
    other = 1 - c
    swp = xl * ((c + xh) % 2)
    vc = (c + swp) % 2
    vxh = (xh + swp) % 2
    swapped = swp == 1

    def at(c_=None, x_=None, y_=None, z_=None):
        x_ = x if x_ is None else x_
        return (
            x_ % 2,
            c if c_ is None else c_,
            y if y_ is None else y_,
            x_ // 2,
            z if z_ is None else z_,
        )

    xq = 2 * vxh + xl
    yo = [(y + j) % NY for j in range(NY)]
    zo = [(z + j) % NZ for j in range(NZ)]
    xo = [(x + j) % NX for j in range(NX)]
    cx = [(c if i == 0 else other, xo[j]) for i in range(2) for j in range(NX)]
    yz = [(yo[i], zo[j]) for i in range(NY) for j in range(NZ)]
    own = pl.ds(pl.multiple_of(c * ROWS, ROWS), ROWS)
    oth = pl.ds(pl.multiple_of(other * ROWS, ROWS), ROWS)
    relays = x % 2 == 0

    def rdma(src, dst, ss, rs, dev):
        return pltpu.make_async_remote_copy(
            src_ref=src, dst_ref=dst, send_sem=ss, recv_sem=rs, device_id=dev,
            device_id_type=pl.DeviceIdType.MESH,
        )

    load = pltpu.make_async_copy(points, pv, r_pv)
    load.start()
    lf_remote = rdma(lf_in, lf, s_lf, r_lf, at(c_=vc, x_=xq))
    lf_local = pltpu.make_async_copy(lf_in, lf, r_lf)
    order = [yo[2], yo[1], yo[3], yo[0]]

    def cols(h, b, r, n):
        return points.at[pl.ds(r, n), pl.ds(pl.multiple_of(h * HALF + b * YB, YB), YB)]

    def half_local(b):
        return pltpu.make_async_copy(cols(c, b, 0, ROWS), pts.at[b, own], r_pts.at[b, c])

    def half_out(b):
        return rdma(cols(other, b, 0, ROWS), pts.at[b, own], s_pts.at[0, b], r_pts.at[b, c],
                    at(c_=other))

    def piece(j, h, r):
        return rdma(cols(h, order[j], r * 128, 128), relay.at[r, j], s_rel.at[h, r, j],
                    r_rel.at[r, j], at(c_=h, x_=xo[1] if r == 0 else xo[3]))

    def forward(j, r):
        to = xo[1] if r == 0 else xo[3]
        slot = (3 - to) // 2
        rows = pl.ds(pl.multiple_of(slot * ROWS + r * 128, 128), 128)
        return rdma(relay.at[r, j], pts.at[order[j], rows], s_fwd.at[r, j],
                    r_pts.at[order[j], slot], at(x_=to))

    @pl.when(jnp.logical_not(swapped))
    def _():
        lf_local.start()
        for b in order:
            half_local(b).start()

    barrier = pltpu.get_barrier_semaphore()
    peers = [at(c_=a, x_=b) for a, b in cx[1:]] + [at(y_=a, z_=b) for a, b in yz[1:]]
    for p in peers:
        pl.semaphore_signal(barrier, inc=1, device_id=p, device_id_type=pl.DeviceIdType.MESH)
    pl.semaphore_wait(barrier, len(peers))

    @pl.when(swapped)
    def _():
        lf_remote.start()
        for j in range(NY):
            for r in range(2):
                for h in range(2):
                    piece(j, h, r).start()

    @pl.when(jnp.logical_not(swapped))
    def _():
        for b in order:
            half_out(b).start()

    load.wait()
    squares = jnp.zeros((ROWS, 1), jnp.float32)
    for k in range(8):
        part_k = pv[:, k * 256 : (k + 1) * 256]
        squares += jnp.sum(part_k * part_k, axis=1, keepdims=True)
    squares_row = jnp.transpose(jnp.broadcast_to(squares, (ROWS, 128)))[:8]
    row = lax.broadcasted_iota(jnp.int32, (8, ROWS), 0)
    meta_out[...] = jnp.where(
        row == 0, squares_row, jnp.where(row == 1, 1.0, jnp.where(row == 2, mass[...], 0.0))
    )
    meta_remote = rdma(meta_out, meta.at[vc], s_meta.at[0], r_meta.at[vc],
                       at(c_=other, x_=xq))
    meta_own = rdma(meta_out, meta.at[vc], s_meta.at[1], r_meta.at[vc], at(c_=c, x_=xq))
    meta_local = pltpu.make_async_copy(meta_out, meta.at[vc], r_meta.at[vc])
    meta_remote.start()

    @pl.when(swapped)
    def _():
        meta_own.start()

    @pl.when(jnp.logical_not(swapped))
    def _():
        meta_local.start()

    lf_remote.wait_recv()
    for v in range(2):
        rdma(meta_out, meta.at[v], s_meta.at[0], r_meta.at[v], at(c_=other)).wait_recv()
    percol[...] = jnp.transpose(meta[c])

    def wait_points(b):
        for v in range(2):
            dst = pts.at[b, pl.ds(v * ROWS, ROWS)]
            rdma(dst, dst, s_pts.at[0, b], r_pts.at[b, v], at(c_=other)).wait_recv()

    def step(it, _):
        v = lf[...]
        e = jnp.exp(v - jnp.max(v, axis=1, keepdims=True))
        mass_own = percol[:, 2:3]
        scaled[it, own] = e / jnp.sum(e, axis=1, keepdims=True) * mass_own
        cp = rdma(scaled.at[it, own], scaled.at[it, own], s_sc.at[it], r_sc.at[it], at(c_=other))
        cp.start()
        cp.wait_send()
        rdma(scaled.at[it, oth], scaled.at[it, oth], s_sc.at[it], r_sc.at[it],
             at(c_=other)).wait_recv()

        stat[it, 0] = dot1(meta[0], scaled[it, :ROWS]) + dot1(meta[1], scaled[it, ROWS:])
        st = [rdma(stat.at[it, 0], stat.at[it, j], s_st.at[it, j], r_st.at[it, j], at(y_=yo[j]))
              for j in range(1, NY)]
        for cpy in st:
            cpy.start()

        def moment(j):
            @pl.when(it == 0)
            def _():
                @pl.when(relays)
                def _():
                    for r in range(2):
                        piece(j, c, r).wait_recv()
                        forward(j, r).start()
                wait_points(order[j])
            return dot0(pts[order[j]], scaled[it])

        mom[it, 2] = moment(0)
        up1 = rdma(mom.at[it, 2, pl.ds(0, 128)], ring1.at[it, 0], s_r1.at[it, 0],
                   r_r1.at[it, 0], at(y_=yo[1]))
        dn1 = rdma(mom.at[it, 2, pl.ds(128, 128)], ring1.at[it, 1], s_r1.at[it, 1],
                   r_r1.at[it, 1], at(y_=yo[3]))
        up1.start()
        dn1.start()
        m1 = moment(1)
        up1.wait_recv()
        mom[it, 1, :128] = m1[:128] + ring1[it, 0]
        mom[it, 1, 128:] = m1[128:]
        up2 = rdma(mom.at[it, 1], ring2.at[it, 0], s_r2.at[it, 0], r_r2.at[it, 0], at(y_=yo[1]))
        up2.start()
        m3 = moment(2)
        dn1.wait_recv()
        mom[it, 3, :128] = m3[:128]
        mom[it, 3, 128:] = m3[128:] + ring1[it, 1]
        dn2 = rdma(mom.at[it, 3], ring2.at[it, 1], s_r2.at[it, 1], r_r2.at[it, 1], at(y_=yo[3]))
        dn2.start()
        mom[it, 0] = moment(3)
        for cpy in st:
            cpy.wait_recv()
        stats_y = stat[it, 0] + stat[it, 1] + stat[it, 2] + stat[it, 3]
        for k in range(NZ):
            zsend[it, k, ZB:] = stats_y
        up2.wait_recv()
        dn2.wait_recv()
        for k in range(NZ):
            r = slice(k * ZB, (k + 1) * ZB)
            zsend[it, k, :ZB] = mom[it, 0, r] + ring2[it, 0, r] + ring2[it, 1, r]

        zc = [rdma(zsend.at[it, zo[j]], zrecv.at[it, j], s_z.at[it, j], r_z.at[it, j],
                   at(z_=zo[j])) for j in range(1, NZ)]
        for cpy in zc:
            cpy.start()
        shard = zsend[it, z]
        for j in range(1, NZ):
            zc[j - 1].wait_recv()
            shard += zrecv[it, j]

        xall[it, x] = shard
        xc = [rdma(xall.at[it, x], xall.at[it, x], s_x.at[it, j], r_x.at[it, j], at(x_=xo[j]))
              for j in range(1, NX)]
        for cpy in xc:
            cpy.start()
        for j in range(1, NX):
            xm = (x + NX - j) % NX
            rdma(xall.at[it, xm], xall.at[it, xm], s_x.at[it, j], r_x.at[it, j],
                 at(x_=xo[j])).wait_recv()
        source = xall[it, 0] + xall[it, 1] + xall[it, 2]
        target = xall[it, 3]
        is_target = x == 3
        facing = jnp.where(is_target, source, target)

        zrows = pl.ds(pl.multiple_of(z * ZB, ZB), ZB)
        gath[it, y, zrows] = facing[:ZB]
        gz = [rdma(gath.at[it, y, zrows], gath.at[it, y, zrows], s_gz.at[it, j], r_gz.at[it, j],
                   at(z_=zo[j])) for j in range(1, NZ)]
        for cpy in gz:
            cpy.start()
        source_mass = jnp.sum(source[ZB + 1 : ZB + 2])
        target_mass = jnp.sum(target[ZB + 1 : ZB + 2])
        facing_mass = jnp.where(is_target, source_mass, target_mass)
        marginal = 0.5 * (source[ZB + 1 : ZB + 2] / source_mass
                          + target[ZB + 1 : ZB + 2] / target_mass)
        for j in range(1, NZ):
            zr = pl.ds(pl.multiple_of(((z + NZ - j) % NZ) * ZB, ZB), ZB)
            rdma(gath.at[it, y, zr], gath.at[it, y, zr], s_gz.at[it, j], r_gz.at[it, j],
                 at(z_=zo[j])).wait_recv()
        gu1 = rdma(gath.at[it, y], gath.at[it, y], s_gy.at[it, 0], r_gy.at[it, 0], at(y_=yo[1]))
        gd1 = rdma(gath.at[it, y], gath.at[it, y], s_gy.at[it, 1], r_gy.at[it, 1], at(y_=yo[3]))
        gu1.start()
        gd1.start()
        acc[...] = dot1(pts[y], gath[it, y])

        def got(b, rows, k):
            r = gath.at[it, b, rows]
            rdma(r, r, s_gy.at[it, k], r_gy.at[it, k], at(y_=yo[1])).wait_recv()

        whole, lo, hi = pl.ds(0, YB), pl.ds(0, 128), pl.ds(128, 128)
        got(yo[3], whole, 0)
        gu2 = rdma(gath.at[it, yo[3], lo], gath.at[it, yo[3], lo], s_gy.at[it, 2],
                   r_gy.at[it, 2], at(y_=yo[1]))
        gu2.start()
        got(yo[1], whole, 1)
        gd2 = rdma(gath.at[it, yo[1], hi], gath.at[it, yo[1], hi], s_gy.at[it, 3],
                   r_gy.at[it, 3], at(y_=yo[3]))
        gd2.start()
        acc[...] += dot1(pts[yo[3]], gath[it, yo[3]])
        acc[...] += dot1(pts[yo[1]], gath[it, yo[1]])
        got(yo[2], lo, 2)
        got(yo[2], hi, 3)
        part[it, 0] = acc[oth] + dot1(pts[yo[2], oth], gath[it, yo[2]])
        pc = rdma(part.at[it, 0], part.at[it, 1], s_pt.at[it], r_pt.at[it], at(c_=other))
        pc.start()
        cross = acc[own] + dot1(pts[yo[2], own], gath[it, yo[2]])
        pc.wait_recv()
        cross += part[it, 1]

        facing_columns = facing[ZB + 1 : ZB + 2]
        facing_norms = facing[ZB : ZB + 1]
        squares_own = percol[:, 0:1]
        g = (
            squares_own * (facing_columns / facing_mass)
            - 2.0 * (cross / facing_mass)
            + facing_norms / facing_mass
        ) / marginal
        grad[...] = g
        centred = g - jnp.sum(g, axis=1, keepdims=True) * (1.0 / RANK)
        largest = jnp.max(jnp.abs(centred))

        last = it == ITERS - 1

        @pl.when(last)
        def _():
            @pl.when(swapped)
            def _():
                rdma(lf, fin.at[0], s_fin.at[0], r_fin.at[0], at(c_=vc, x_=xq)).start()
                rdma(grad, fin.at[1], s_fin.at[1], r_fin.at[1], at(c_=vc, x_=xq)).start()

        tile = (8, 128)
        mx[it, 0] = jnp.full(tile, largest)
        mc = [rdma(mx.at[it, 0], mx.at[it, j], s_mc.at[it, j], r_mc.at[it, j],
                   at(c_=cx[j][0], x_=cx[j][1])) for j in range(1, 8)]
        for cpy in mc:
            cpy.start()
        m = mx[it, 0]
        for j in range(1, 8):
            mc[j - 1].wait_recv()
        for j in range(1, 8):
            m = jnp.maximum(m, mx[it, j])
        mx[it, 8] = m
        my = [rdma(mx.at[it, 8], mx.at[it, 8 + j], s_my.at[it, j], r_my.at[it, j],
                   at(y_=yz[j][0], z_=yz[j][1])) for j in range(1, NY * NZ)]
        for cpy in my:
            cpy.start()
        for cpy in my:
            cpy.wait_recv()
        for j in range(1, NY * NZ):
            m = jnp.maximum(m, mx[it, 8 + j])
        rate = STEP_SCALE / (m[0:1, 0:1] + 1e-6)

        @pl.when(jnp.logical_not(last))
        def _():
            lf[...] = lf[...] - rate * grad[...]

        @pl.when(last)
        def _():
            def finish(a, b):
                u = a - rate * b
                ex = jnp.exp(u - jnp.max(u, axis=1, keepdims=True))
                out[...] = ex / jnp.sum(ex, axis=1, keepdims=True)

            @pl.when(swapped)
            def _():
                for k, src in ((0, lf), (1, grad)):
                    cpy = rdma(src, fin.at[k], s_fin.at[k], r_fin.at[k], at(c_=vc, x_=xq))
                    cpy.wait_send()
                    cpy.wait_recv()
                finish(fin[0], fin[1])

            @pl.when(jnp.logical_not(swapped))
            def _():
                finish(lf[...], grad[...])

        for cpy in [up1, dn1, up2, dn2, gu1, gd1, gu2, gd2, pc] + st + zc + xc + gz + mc + my:
            cpy.wait_send()
        return 0

    lax.fori_loop(0, ITERS, step, 0)

    meta_remote.wait_send()

    @pl.when(swapped)
    def _():
        lf_remote.wait_send()
        meta_own.wait_send()
        for j in range(NY):
            for r in range(2):
                for h in range(2):
                    piece(j, h, r).wait_send()

    @pl.when(jnp.logical_not(swapped))
    def _():
        for b in order:
            half_out(b).wait_send()

    @pl.when(relays)
    def _():
        for j in range(NY):
            for r in range(2):
                forward(j, r).wait_send()


def body(points, log_factor, masses):
    mass = masses.reshape(1, ROWS)
    f32 = jnp.float32
    vm = lambda *s: pltpu.VMEM(s, f32)
    dma = lambda *s: pltpu.SemaphoreType.DMA(s)
    n = ITERS
    share = pl.pallas_call(
        kernel,
        out_shape=jax.ShapeDtypeStruct((ROWS, RANK), f32),
        in_specs=[pl.BlockSpec(memory_space=pltpu.HBM)] * 2
        + [pl.BlockSpec(memory_space=pltpu.VMEM)],
        out_specs=pl.BlockSpec(memory_space=pltpu.VMEM),
        scratch_shapes=[
            vm(NY, 2 * ROWS, YB), vm(ROWS, 2 * HALF), vm(2, NY, 128, YB), vm(ROWS, RANK),
            vm(2, 8, ROWS), vm(8, ROWS), vm(ROWS, 8),
            vm(n, 2 * ROWS, RANK), vm(n, NY, YB, RANK), vm(n, 2, 128, RANK), vm(n, 2, YB, RANK),
            vm(n, NY, 8, RANK), vm(n, NZ, ZS, RANK), vm(n, NZ, ZS, RANK), vm(n, NX, ZS, RANK),
            vm(n, NY, YB, RANK), vm(2 * ROWS, RANK), vm(n, 2, ROWS, RANK),
            vm(n, 40, 8, 128), vm(ROWS, RANK), vm(2, ROWS, RANK),
            pltpu.SemaphoreType.DMA, dma(2, 2, NY), dma(2, NY), dma(2, NY),
            dma(2, NY), dma(NY, 2), pltpu.SemaphoreType.DMA, pltpu.SemaphoreType.DMA,
            dma(2), dma(2), dma(n), dma(n), dma(n, 2), dma(n, 2), dma(n, 2), dma(n, 2),
            dma(n, NY), dma(n, NY), dma(n, NZ), dma(n, NZ), dma(n, NX), dma(n, NX),
            dma(n, NZ), dma(n, NZ), dma(n, 4), dma(n, 4), dma(n), dma(n),
            dma(n, 8), dma(n, 8), dma(n, NY * NZ), dma(n, NY * NZ),
            dma(2), dma(2),
        ],
        compiler_params=pltpu.CompilerParams(
            collective_id=0, has_side_effects=True, vmem_limit_bytes=62 << 20
        ),
        name="steps",
    )(points, log_factor, mass)
    return RANK * share


def solution(mesh):
    split = Mesh(mesh.devices.reshape(2, 2, 4, 2, 8), AXES)
    rows = ("xl", "c", "y", "xh", "z")
    return jax.shard_map(
        body,
        mesh=split,
        in_specs=(P(rows, None), P(rows, None), P(rows)),
        out_specs=P(rows, None),
        check_vma=False,
    )
```

```python
import functools

import jax
import jax.numpy as jnp
from jax import lax
from jax.experimental import pallas as pl
from jax.experimental.pallas import tpu as pltpu
from jax.sharding import Mesh
from jax.sharding import PartitionSpec as P

ITERS = 2
STEP_SCALE = 4.0
AXES = ("xl", "c", "y", "xh", "z")
NY, NZ, NX = 4, 8, 4
ROWS = 256
RANK = 256
HALF = 1024
YB = HALF // NY
ZB = YB // NZ
ZS = ZB + 8
HIGHEST = lax.Precision.HIGHEST


def dot0(a, b):
    return lax.dot_general(
        a, b, (((0,), (0,)), ((), ())), precision=HIGHEST, preferred_element_type=jnp.float32
    )


def dot1(a, b):
    return lax.dot_general(
        a, b, (((1,), (0,)), ((), ())), precision=HIGHEST, preferred_element_type=jnp.float32
    )


def kernel(
    points, lf_in, mass, out,
    pts, pv, relay, lf, meta, meta_out, percol, scaled, mom, ring1, ring2, stat, zsend, zrecv, xall, gath, acc, part,
    mx, grad, fin,
    r_pv, s_rel, r_rel, s_fwd, s_pts, r_pts, s_lf, r_lf, s_meta, r_meta, s_sc, r_sc, s_r, r_r, s_st, r_st,
    s_z, r_z, s_x, r_x, s_gz, r_gz, s_gy, r_gy, s_pt, r_pt, s_mc, r_mc, s_my, r_my,
    s_fin, r_fin,
):
    xl, c, y, xh, z = (lax.axis_index(a) for a in AXES)
    x = 2 * xh + xl
    other = 1 - c
    swp = xl * ((c + xh) % 2)
    vc = (c + swp) % 2
    vxh = (xh + swp) % 2
    swapped = swp == 1

    def at(c_=None, x_=None, y_=None, z_=None):
        x_ = x if x_ is None else x_
        return (
            x_ % 2,
            c if c_ is None else c_,
            y if y_ is None else y_,
            x_ // 2,
            z if z_ is None else z_,
        )

    xq = 2 * vxh + xl
    yo = [(y + j) % NY for j in range(NY)]
    zo = [(z + j) % NZ for j in range(NZ)]
    xo = [(x + j) % NX for j in range(NX)]
    cx = [(c if i == 0 else other, xo[j]) for i in range(2) for j in range(NX)]
    yz = [(yo[i], zo[j]) for i in range(NY) for j in range(NZ)]
    own = pl.ds(pl.multiple_of(c * ROWS, ROWS), ROWS)
    oth = pl.ds(pl.multiple_of(other * ROWS, ROWS), ROWS)
    relays = x % 2 == 0

    def rdma(src, dst, ss, rs, dev):
        return pltpu.make_async_remote_copy(
            src_ref=src, dst_ref=dst, send_sem=ss, recv_sem=rs, device_id=dev,
            device_id_type=pl.DeviceIdType.MESH,
        )

    def sent(ref, sem):
        rdma(ref, ref, sem, sem, at(c_=other)).wait_send()

    def arrived(ref, sem):
        rdma(ref, ref, sem, sem, at(c_=other)).wait_recv()

    load = pltpu.make_async_copy(points, pv, r_pv)
    load.start()
    lf_remote = rdma(lf_in, lf, s_lf, r_lf, at(c_=vc, x_=xq))
    lf_local = pltpu.make_async_copy(lf_in, lf, r_lf)
    order = [yo[2], yo[1], yo[3], yo[0]]

    def cols(h, b, r, n):
        return points.at[pl.ds(r, n), pl.ds(pl.multiple_of(h * HALF + b * YB, YB), YB)]

    def half_local(b):
        return pltpu.make_async_copy(cols(c, b, 0, ROWS), pts.at[b, own], r_pts.at[b, c])

    def half_out(b):
        return rdma(cols(other, b, 0, ROWS), pts.at[b, own], s_pts.at[0, b], r_pts.at[b, c],
                    at(c_=other))

    def piece(j, h, r):
        return rdma(cols(h, order[j], r * 128, 128), relay.at[r, j], s_rel.at[h, r, j],
                    r_rel.at[r, j], at(c_=h, x_=xo[1] if r == 0 else xo[3]))

    def forward(j, r):
        to = xo[1] if r == 0 else xo[3]
        slot = (3 - to) // 2
        rows = pl.ds(pl.multiple_of(slot * ROWS + r * 128, 128), 128)
        return rdma(relay.at[r, j], pts.at[order[j], rows], s_fwd.at[r, j],
                    r_pts.at[order[j], slot], at(x_=to))

    @pl.when(jnp.logical_not(swapped))
    def _():
        lf_local.start()
        for b in order:
            half_local(b).start()

    barrier = pltpu.get_barrier_semaphore()
    peers = [at(c_=a, x_=b) for a, b in cx[1:]] + [at(y_=a, z_=b) for a, b in yz[1:]]
    for p in peers:
        pl.semaphore_signal(barrier, inc=1, device_id=p, device_id_type=pl.DeviceIdType.MESH)

    load.wait()
    squares = jnp.zeros((ROWS, 1), jnp.float32)
    for k in range(8):
        part_k = pv[:, k * 256 : (k + 1) * 256]
        squares += jnp.sum(part_k * part_k, axis=1, keepdims=True)
    squares_row = jnp.transpose(jnp.broadcast_to(squares, (ROWS, 128)))[:8]
    row = lax.broadcasted_iota(jnp.int32, (8, ROWS), 0)
    meta_out[...] = jnp.where(
        row == 0, squares_row, jnp.where(row == 1, 1.0, jnp.where(row == 2, mass[...], 0.0))
    )
    pl.semaphore_wait(barrier, len(peers))

    meta_remote = rdma(meta_out, meta.at[vc], s_meta.at[0], r_meta.at[vc],
                       at(c_=other, x_=xq))
    meta_own = rdma(meta_out, meta.at[vc], s_meta.at[1], r_meta.at[vc], at(c_=c, x_=xq))
    meta_local = pltpu.make_async_copy(meta_out, meta.at[vc], r_meta.at[vc])
    meta_remote.start()

    @pl.when(swapped)
    def _():
        meta_own.start()

    @pl.when(jnp.logical_not(swapped))
    def _():
        meta_local.start()

    @pl.when(swapped)
    def _():
        lf_remote.start()
        for j in range(NY):
            for r in range(2):
                for h in range(2):
                    piece(j, h, r).start()

    @pl.when(jnp.logical_not(swapped))
    def _():
        for b in order:
            half_out(b).start()

    lf_remote.wait_recv()
    for v in range(2):
        rdma(meta_out, meta.at[v], s_meta.at[0], r_meta.at[v], at(c_=other)).wait_recv()
    percol[...] = jnp.transpose(meta[c])

    def wait_points(b):
        for v in range(2):
            dst = pts.at[b, pl.ds(v * ROWS, ROWS)]
            rdma(dst, dst, s_pts.at[0, b], r_pts.at[b, v], at(c_=other)).wait_recv()

    def step(it, _):
        v = lf[...]
        e = jnp.exp(v - jnp.max(v, axis=1, keepdims=True))
        mass_own = percol[:, 2:3]
        scaled[it, own] = e / jnp.sum(e, axis=1, keepdims=True) * mass_own
        cp = rdma(scaled.at[it, own], scaled.at[it, own], s_sc.at[it], r_sc.at[it], at(c_=other))
        cp.start()

        def ready(j):
            @pl.when(it == 0)
            def _():
                @pl.when(relays)
                def _():
                    for r in range(2):
                        piece(j, c, r).wait_recv()
                        forward(j, r).start()
                wait_points(order[j])

        def moment(j):
            ready(j)
            return dot0(pts[order[j]], scaled[it])

        lo, hi = pl.ds(0, 128), pl.ds(128, 128)
        up, dn = at(y_=yo[1]), at(y_=yo[3])
        ready(0)
        mom[it, 2] = dot0(pts[order[0], own], scaled[it, own])
        arrived(scaled.at[it, oth], r_sc.at[it])
        mom[it, 2] += dot0(pts[order[0], oth], scaled[it, oth])

        def ring(k, rows, dst, n, dev):
            cpy = rdma(mom.at[it, k, rows], dst, s_r.at[it, n], r_r.at[it, n], dev)
            cpy.start()
            return cpy

        up1 = ring(2, lo, ring1.at[it, 0], 0, up)
        dn1 = ring(2, hi, ring1.at[it, 1], 1, dn)
        mom[it, 1] = moment(1)
        up2 = ring(1, hi, ring2.at[it, 0, hi], 2, up)
        mom[it, 3] = moment(2)
        dn2 = ring(3, lo, ring2.at[it, 1, lo], 3, dn)
        up1.wait_recv()
        mom[it, 1, lo] += ring1[it, 0]
        up3 = ring(1, lo, ring2.at[it, 0, lo], 4, up)
        dn1.wait_recv()
        mom[it, 3, hi] += ring1[it, 1]
        dn3 = ring(3, hi, ring2.at[it, 1, hi], 5, dn)

        stat[it, 0] = dot1(meta[0], scaled[it, :ROWS]) + dot1(meta[1], scaled[it, ROWS:])
        for j in range(1, NY):
            rdma(stat.at[it, 0], stat.at[it, j], s_st.at[it], r_st.at[it], at(y_=yo[j])).start()
        mom[it, 0] = moment(3)
        arrived(stat.at[it, pl.ds(1, NY - 1)], r_st.at[it])
        stats_y = stat[it, 0] + stat[it, 1] + stat[it, 2] + stat[it, 3]
        for k in range(NZ):
            zsend[it, k, ZB:] = stats_y
        for cpy in (up2, dn2, up3, dn3):
            cpy.wait_recv()
        for k in range(NZ):
            r = slice(k * ZB, (k + 1) * ZB)
            zsend[it, k, :ZB] = mom[it, 0, r] + ring2[it, 0, r] + ring2[it, 1, r]

        for j in range(1, NZ):
            rdma(zsend.at[it, zo[j]], zrecv.at[it, j], s_z.at[it], r_z.at[it],
                 at(z_=zo[j])).start()
        arrived(zrecv.at[it, pl.ds(1, NZ - 1)], r_z.at[it])
        shard = zsend[it, z]
        for j in range(1, NZ):
            shard += zrecv[it, j]

        xall[it, x] = shard
        for j in range(1, NX):
            rdma(xall.at[it, x], xall.at[it, x], s_x.at[it], r_x.at[it], at(x_=xo[j])).start()
        arrived(xall.at[it, pl.ds(0, NX - 1)], r_x.at[it])
        source = xall[it, 0] + xall[it, 1] + xall[it, 2]
        target = xall[it, 3]
        is_target = x == 3
        facing = jnp.where(is_target, source, target)

        zrows = pl.ds(pl.multiple_of(z * ZB, ZB), ZB)
        gath[it, y, zrows] = facing[:ZB]
        for j in range(1, NZ):
            rdma(gath.at[it, y, zrows], gath.at[it, y, zrows], s_gz.at[it], r_gz.at[it],
                 at(z_=zo[j])).start()
        source_mass = jnp.sum(source[ZB + 1 : ZB + 2])
        target_mass = jnp.sum(target[ZB + 1 : ZB + 2])
        facing_mass = jnp.where(is_target, source_mass, target_mass)
        marginal = 0.5 * (source[ZB + 1 : ZB + 2] / source_mass
                          + target[ZB + 1 : ZB + 2] / target_mass)
        arrived(gath.at[it, y, pl.ds(0, (NZ - 1) * ZB)], r_gz.at[it])

        def block(b, rows, n, dev):
            ref = gath.at[it, b, rows]
            return rdma(ref, ref, s_gy.at[it, n], r_gy.at[it, n], dev)

        gout = [block(y, lo, 0, up), block(y, hi, 1, dn), block(y, hi, 2, up),
                block(y, lo, 3, dn)]
        for cpy in gout:
            cpy.start()
        acc[...] = dot1(pts[y], gath[it, y])
        block(yo[3], lo, 0, up).wait_recv()
        gout += [block(yo[3], lo, 4, up)]
        gout[4].start()
        block(yo[1], hi, 1, dn).wait_recv()
        gout += [block(yo[1], hi, 5, dn)]
        gout[5].start()
        block(yo[3], hi, 2, up).wait_recv()
        acc[...] += dot1(pts[yo[3]], gath[it, yo[3]])
        block(yo[1], lo, 3, dn).wait_recv()
        acc[...] += dot1(pts[yo[1]], gath[it, yo[1]])
        block(yo[2], lo, 4, up).wait_recv()
        block(yo[2], hi, 5, dn).wait_recv()
        part[it, 0] = acc[oth] + dot1(pts[yo[2], oth], gath[it, yo[2]])
        pc = rdma(part.at[it, 0], part.at[it, 1], s_pt.at[it], r_pt.at[it], at(c_=other))
        pc.start()
        cross = acc[own] + dot1(pts[yo[2], own], gath[it, yo[2]])
        pc.wait_recv()
        cross += part[it, 1]

        facing_columns = facing[ZB + 1 : ZB + 2]
        facing_norms = facing[ZB : ZB + 1]
        squares_own = percol[:, 0:1]
        g = (
            squares_own * (facing_columns / facing_mass)
            - 2.0 * (cross / facing_mass)
            + facing_norms / facing_mass
        ) / marginal
        grad[...] = g
        centred = g - jnp.sum(g, axis=1, keepdims=True) * (1.0 / RANK)
        largest = jnp.max(jnp.abs(centred))

        last = it == ITERS - 1

        @pl.when(last)
        def _():
            @pl.when(swapped)
            def _():
                rdma(lf, fin.at[0], s_fin.at[0], r_fin.at[0], at(c_=vc, x_=xq)).start()
                rdma(grad, fin.at[1], s_fin.at[1], r_fin.at[1], at(c_=vc, x_=xq)).start()

        tile = (8, 128)
        mx[it, 0] = jnp.full(tile, largest)
        for j in range(1, 8):
            rdma(mx.at[it, 0], mx.at[it, j], s_mc.at[it], r_mc.at[it],
                 at(c_=cx[j][0], x_=cx[j][1])).start()
        for cpy in [cp, up1, dn1, up2, dn2, up3, dn3]:
            cpy.wait_send()
        sent(stat.at[it, pl.ds(1, NY - 1)], s_st.at[it])
        sent(zrecv.at[it, pl.ds(1, NZ - 1)], s_z.at[it])
        arrived(mx.at[it, pl.ds(1, 7)], r_mc.at[it])
        mx[it, 8] = jnp.max(mx[it, :8], axis=0)
        for j in range(1, NY * NZ):
            rdma(mx.at[it, 8], mx.at[it, 8 + j], s_my.at[it], r_my.at[it],
                 at(y_=yz[j][0], z_=yz[j][1])).start()
        sent(xall.at[it, pl.ds(0, NX - 1)], s_x.at[it])
        sent(gath.at[it, y, pl.ds(0, (NZ - 1) * ZB)], s_gz.at[it])
        for cpy in gout + [pc]:
            cpy.wait_send()
        sent(mx.at[it, pl.ds(1, 7)], s_mc.at[it])
        arrived(mx.at[it, pl.ds(9, NY * NZ - 1)], r_my.at[it])
        m = jnp.max(mx[it, 8:40], axis=0)
        rate = STEP_SCALE / (m[0:1, 0:1] + 1e-6)

        @pl.when(jnp.logical_not(last))
        def _():
            lf[...] = lf[...] - rate * grad[...]

        @pl.when(last)
        def _():
            def finish(a, b):
                u = a - rate * b
                ex = jnp.exp(u - jnp.max(u, axis=1, keepdims=True))
                out[...] = ex / jnp.sum(ex, axis=1, keepdims=True)

            @pl.when(swapped)
            def _():
                for k, src in ((0, lf), (1, grad)):
                    cpy = rdma(src, fin.at[k], s_fin.at[k], r_fin.at[k], at(c_=vc, x_=xq))
                    cpy.wait_send()
                    cpy.wait_recv()
                finish(fin[0], fin[1])

            @pl.when(jnp.logical_not(swapped))
            def _():
                finish(lf[...], grad[...])

        sent(mx.at[it, pl.ds(9, NY * NZ - 1)], s_my.at[it])
        return 0

    lax.fori_loop(0, ITERS, step, 0)

    meta_remote.wait_send()

    @pl.when(swapped)
    def _():
        lf_remote.wait_send()
        meta_own.wait_send()
        for j in range(NY):
            for r in range(2):
                for h in range(2):
                    piece(j, h, r).wait_send()

    @pl.when(jnp.logical_not(swapped))
    def _():
        for b in order:
            half_out(b).wait_send()

    @pl.when(relays)
    def _():
        for j in range(NY):
            for r in range(2):
                forward(j, r).wait_send()


def body(points, log_factor, masses):
    mass = masses.reshape(1, ROWS)
    f32 = jnp.float32
    vm = lambda *s: pltpu.VMEM(s, f32)
    dma = lambda *s: pltpu.SemaphoreType.DMA(s)
    n = ITERS
    share = pl.pallas_call(
        kernel,
        out_shape=jax.ShapeDtypeStruct((ROWS, RANK), f32),
        in_specs=[pl.BlockSpec(memory_space=pltpu.HBM)] * 2
        + [pl.BlockSpec(memory_space=pltpu.VMEM)],
        out_specs=pl.BlockSpec(memory_space=pltpu.VMEM),
        scratch_shapes=[
            vm(NY, 2 * ROWS, YB), vm(ROWS, 2 * HALF), vm(2, NY, 128, YB), vm(ROWS, RANK),
            vm(2, 8, ROWS), vm(8, ROWS), vm(ROWS, 8),
            vm(n, 2 * ROWS, RANK), vm(n, NY, YB, RANK), vm(n, 2, 128, RANK), vm(n, 2, YB, RANK),
            vm(n, NY, 8, RANK), vm(n, NZ, ZS, RANK), vm(n, NZ, ZS, RANK), vm(n, NX, ZS, RANK),
            vm(n, NY, YB, RANK), vm(2 * ROWS, RANK), vm(n, 2, ROWS, RANK),
            vm(n, 40, 8, 128), vm(ROWS, RANK), vm(2, ROWS, RANK),
            pltpu.SemaphoreType.DMA, dma(2, 2, NY), dma(2, NY), dma(2, NY),
            dma(2, NY), dma(NY, 2), pltpu.SemaphoreType.DMA, pltpu.SemaphoreType.DMA,
            dma(2), dma(2), dma(n), dma(n), dma(n, 6), dma(n, 6), dma(n), dma(n),
            dma(n), dma(n), dma(n), dma(n), dma(n), dma(n), dma(n, 6), dma(n, 6),
            dma(n), dma(n), dma(n), dma(n), dma(n), dma(n), dma(2), dma(2),
        ],
        compiler_params=pltpu.CompilerParams(
            collective_id=0, has_side_effects=True, vmem_limit_bytes=62 << 20
        ),
        name="steps",
    )(points, log_factor, mass)
    return RANK * share


def solution(mesh):
    split = Mesh(mesh.devices.reshape(2, 2, 4, 2, 8), AXES)
    rows = ("xl", "c", "y", "xh", "z")
    return jax.shard_map(
        body,
        mesh=split,
        in_specs=(P(rows, None), P(rows, None), P(rows)),
        out_specs=P(rows, None),
        check_vma=False,
    )
```

```python
import functools

import jax
import jax.numpy as jnp
from jax import lax
from jax.experimental import pallas as pl
from jax.experimental.pallas import tpu as pltpu
from jax.sharding import Mesh
from jax.sharding import PartitionSpec as P

ITERS = 2
STEP_SCALE = 4.0
AXES = ("xl", "c", "y", "xh", "z")
NY, NZ, NX = 4, 8, 4
ROWS = 256
RANK = 256
HALF = 1024
YB = HALF // NY
ZB = YB // NZ
ZS = ZB + 8
HIGHEST = lax.Precision.HIGHEST


def dot0(a, b):
    return lax.dot_general(
        a, b, (((0,), (0,)), ((), ())), precision=HIGHEST, preferred_element_type=jnp.float32
    )


def dot1(a, b):
    return lax.dot_general(
        a, b, (((1,), (0,)), ((), ())), precision=HIGHEST, preferred_element_type=jnp.float32
    )


def kernel(
    points, lf_in, mass, out,
    pts, pv, relay, lf, meta, meta_out, percol, scaled, mom, ring1, ring2, stat, statz, zsend, zrecv, xall, gath, acc, part,
    mx, grad, fin,
    r_pv, s_rel, r_rel, s_fwd, s_pts, r_pts, s_lf, r_lf, s_meta, r_meta, s_sc, r_sc, s_r, r_r, s_st, r_st,
    s_z, r_z, s_x, r_x, s_gz, r_gz, s_gy, r_gy, s_pt, r_pt, s_mc, r_mc, s_my, r_my,
    s_fin, r_fin,
):
    xl, c, y, xh, z = (lax.axis_index(a) for a in AXES)
    x = 2 * xh + xl
    other = 1 - c
    swp = xl * ((c + xh) % 2)
    vc = (c + swp) % 2
    vxh = (xh + swp) % 2
    swapped = swp == 1

    def at(c_=None, x_=None, y_=None, z_=None):
        x_ = x if x_ is None else x_
        return (
            x_ % 2,
            c if c_ is None else c_,
            y if y_ is None else y_,
            x_ // 2,
            z if z_ is None else z_,
        )

    xq = 2 * vxh + xl
    yo = [(y + j) % NY for j in range(NY)]
    zo = [(z + j) % NZ for j in range(NZ)]
    xo = [(x + j) % NX for j in range(NX)]
    cx = [(c if i == 0 else other, xo[j]) for i in range(2) for j in range(NX)]
    yz = [(yo[i], zo[j]) for i in range(NY) for j in range(NZ)]
    own = pl.ds(pl.multiple_of(c * ROWS, ROWS), ROWS)
    oth = pl.ds(pl.multiple_of(other * ROWS, ROWS), ROWS)
    relays = x % 2 == 0

    def rdma(src, dst, ss, rs, dev):
        return pltpu.make_async_remote_copy(
            src_ref=src, dst_ref=dst, send_sem=ss, recv_sem=rs, device_id=dev,
            device_id_type=pl.DeviceIdType.MESH,
        )

    def sent(ref, sem):
        rdma(ref, ref, sem, sem, at(c_=other)).wait_send()

    def arrived(ref, sem):
        rdma(ref, ref, sem, sem, at(c_=other)).wait_recv()

    load = pltpu.make_async_copy(points, pv, r_pv)
    load.start()
    lf_remote = rdma(lf_in, lf, s_lf, r_lf, at(c_=vc, x_=xq))
    lf_local = pltpu.make_async_copy(lf_in, lf, r_lf)
    order = [yo[2], yo[1], yo[3], yo[0]]

    def cols(h, b, r, n):
        return points.at[pl.ds(r, n), pl.ds(pl.multiple_of(h * HALF + b * YB, YB), YB)]

    def half_local(b):
        return pltpu.make_async_copy(cols(c, b, 0, ROWS), pts.at[b, own], r_pts.at[b, c])

    def half_out(b):
        return rdma(cols(other, b, 0, ROWS), pts.at[b, own], s_pts.at[0, b], r_pts.at[b, c],
                    at(c_=other))

    def piece(j, h, r):
        return rdma(cols(h, order[j], r * 128, 128), relay.at[r, j], s_rel.at[h, r, j],
                    r_rel.at[r, j], at(c_=h, x_=xo[1] if r == 0 else xo[3]))

    def forward(j, r):
        to = xo[1] if r == 0 else xo[3]
        slot = (3 - to) // 2
        rows = pl.ds(pl.multiple_of(slot * ROWS + r * 128, 128), 128)
        return rdma(relay.at[r, j], pts.at[order[j], rows], s_fwd.at[r, j],
                    r_pts.at[order[j], slot], at(x_=to))

    @pl.when(jnp.logical_not(swapped))
    def _():
        lf_local.start()
        for b in order:
            half_local(b).start()

    barrier = pltpu.get_barrier_semaphore()
    peers = [at(c_=a, x_=b) for a, b in cx[1:]] + [at(y_=a, z_=b) for a, b in yz[1:]]
    for p in peers:
        pl.semaphore_signal(barrier, inc=1, device_id=p, device_id_type=pl.DeviceIdType.MESH)

    load.wait()
    squares = jnp.zeros((ROWS, 1), jnp.float32)
    for k in range(8):
        part_k = pv[:, k * 256 : (k + 1) * 256]
        squares += jnp.sum(part_k * part_k, axis=1, keepdims=True)
    squares_row = jnp.transpose(jnp.broadcast_to(squares, (ROWS, 128)))[:8]
    row = lax.broadcasted_iota(jnp.int32, (8, ROWS), 0)
    meta_out[...] = jnp.where(
        row == 0, squares_row, jnp.where(row == 1, 1.0, jnp.where(row == 2, mass[...], 0.0))
    )
    pl.semaphore_wait(barrier, len(peers))

    meta_remote = rdma(meta_out, meta.at[vc], s_meta.at[0], r_meta.at[vc],
                       at(c_=other, x_=xq))
    meta_own = rdma(meta_out, meta.at[vc], s_meta.at[1], r_meta.at[vc], at(c_=c, x_=xq))
    meta_local = pltpu.make_async_copy(meta_out, meta.at[vc], r_meta.at[vc])
    meta_remote.start()

    @pl.when(swapped)
    def _():
        meta_own.start()

    @pl.when(jnp.logical_not(swapped))
    def _():
        meta_local.start()

    def each_piece(j, act):
        for r in range(2):
            for h in range(2):
                act(piece(j, h, r))

    def start(cpy):
        cpy.start()

    def wait_send(cpy):
        cpy.wait_send()

    @pl.when(swapped)
    def _():
        lf_remote.start()
        each_piece(0, start)
        lf_remote.wait_send()
        each_piece(1, start)

    @pl.when(jnp.logical_not(swapped))
    def _():
        for b in order:
            half_out(b).start()

    lf_remote.wait_recv()
    for v in range(2):
        rdma(meta_out, meta.at[v], s_meta.at[0], r_meta.at[v], at(c_=other)).wait_recv()
    percol[...] = jnp.transpose(meta[c])

    def wait_points(b):
        for v in range(2):
            dst = pts.at[b, pl.ds(v * ROWS, ROWS)]
            rdma(dst, dst, s_pts.at[0, b], r_pts.at[b, v], at(c_=other)).wait_recv()

    def step(it, _):
        v = lf[...]
        e = jnp.exp(v - jnp.max(v, axis=1, keepdims=True))
        mass_own = percol[:, 2:3]
        scaled[it, own] = e / jnp.sum(e, axis=1, keepdims=True) * mass_own
        cp = rdma(scaled.at[it, own], scaled.at[it, own], s_sc.at[it], r_sc.at[it], at(c_=other))
        cp.start()
        last = it == ITERS - 1

        @pl.when(last)
        def _():
            @pl.when(swapped)
            def _():
                rdma(lf, fin.at[0], s_fin.at[0], r_fin.at[0], at(c_=vc, x_=xq)).start()

        def ready(j):
            @pl.when(it == 0)
            def _():
                @pl.when(relays)
                def _():
                    for r in range(2):
                        piece(j, c, r).wait_recv()
                        forward(j, r).start()

                if j < 2:
                    @pl.when(swapped)
                    def _():
                        each_piece(j, wait_send)
                        each_piece(j + 2, start)

                wait_points(order[j])

        def moment(j):
            ready(j)
            return dot0(pts[order[j]], scaled[it])

        lo, hi = pl.ds(0, 128), pl.ds(128, 128)
        up, dn = at(y_=yo[1]), at(y_=yo[3])
        ready(0)
        mom[it, 2] = dot0(pts[order[0], own], scaled[it, own])
        arrived(scaled.at[it, oth], r_sc.at[it])
        mom[it, 2] += dot0(pts[order[0], oth], scaled[it, oth])

        def ring(k, rows, dst, n, dev):
            cpy = rdma(mom.at[it, k, rows], dst, s_r.at[it, n], r_r.at[it, n], dev)
            cpy.start()
            return cpy

        up1 = ring(2, lo, ring1.at[it, 0], 0, up)
        dn1 = ring(2, hi, ring1.at[it, 1], 1, dn)
        mom[it, 1] = moment(1)
        up2 = ring(1, hi, ring2.at[it, 0, hi], 2, up)
        mom[it, 3] = moment(2)
        dn2 = ring(3, lo, ring2.at[it, 1, lo], 3, dn)
        stat[it, 0] = dot1(meta[0], scaled[it, :ROWS]) + dot1(meta[1], scaled[it, ROWS:])
        for j in range(1, NY):
            rdma(stat.at[it, 0], stat.at[it, j], s_st.at[it, 0], r_st.at[it, 0],
                 at(y_=yo[j])).start()
        up1.wait_recv()
        mom[it, 1, lo] += ring1[it, 0]
        up3 = ring(1, lo, ring2.at[it, 0, lo], 4, up)
        dn1.wait_recv()
        mom[it, 3, hi] += ring1[it, 1]
        dn3 = ring(3, hi, ring2.at[it, 1, hi], 5, dn)

        mom[it, 0] = moment(3)

        arrived(stat.at[it, pl.ds(1, NY - 1)], r_st.at[it, 0])
        statz[it, 0] = stat[it, 0] + stat[it, 1] + stat[it, 2] + stat[it, 3]
        for j in range(1, NZ):
            rdma(statz.at[it, 0], statz.at[it, j], s_st.at[it, 1], r_st.at[it, 1],
                 at(z_=zo[j])).start()
        for cpy in (up2, dn2, up3, dn3):
            cpy.wait_recv()
        for k in range(NZ):
            r = slice(k * ZB, (k + 1) * ZB)
            zsend[it, k] = mom[it, 0, r] + ring2[it, 0, r] + ring2[it, 1, r]

        for j in range(1, NZ):
            rdma(zsend.at[it, zo[j]], zrecv.at[it, j], s_z.at[it], r_z.at[it],
                 at(z_=zo[j])).start()
        arrived(zrecv.at[it, pl.ds(1, NZ - 1)], r_z.at[it])
        shard = zsend[it, z]
        for j in range(1, NZ):
            shard += zrecv[it, j]
        arrived(statz.at[it, pl.ds(1, NZ - 1)], r_st.at[it, 1])

        xall[it, x, :ZB] = shard
        xall[it, x, ZB:] = jnp.sum(statz[it], axis=0)
        for j in range(1, NX):
            rdma(xall.at[it, x], xall.at[it, x], s_x.at[it], r_x.at[it], at(x_=xo[j])).start()
        arrived(xall.at[it, pl.ds(0, NX - 1)], r_x.at[it])
        source = xall[it, 0] + xall[it, 1] + xall[it, 2]
        target = xall[it, 3]
        is_target = x == 3
        facing = jnp.where(is_target, source, target)

        zrows = pl.ds(pl.multiple_of(z * ZB, ZB), ZB)
        gath[it, y, zrows] = facing[:ZB]
        for j in range(1, NZ):
            rdma(gath.at[it, y, zrows], gath.at[it, y, zrows], s_gz.at[it], r_gz.at[it],
                 at(z_=zo[j])).start()
        source_mass = jnp.sum(source[ZB + 1 : ZB + 2])
        target_mass = jnp.sum(target[ZB + 1 : ZB + 2])
        facing_mass = jnp.where(is_target, source_mass, target_mass)
        marginal = 0.5 * (source[ZB + 1 : ZB + 2] / source_mass
                          + target[ZB + 1 : ZB + 2] / target_mass)
        arrived(gath.at[it, y, pl.ds(0, (NZ - 1) * ZB)], r_gz.at[it])

        def block(b, rows, n, dev):
            ref = gath.at[it, b, rows]
            return rdma(ref, ref, s_gy.at[it, n], r_gy.at[it, n], dev)

        gout = [block(y, lo, 0, up), block(y, hi, 1, dn), block(y, hi, 2, up),
                block(y, lo, 3, dn)]
        for cpy in gout:
            cpy.start()
        acc[...] = dot1(pts[y], gath[it, y])
        block(yo[3], lo, 0, up).wait_recv()
        gout += [block(yo[3], lo, 4, up)]
        gout[4].start()
        block(yo[1], hi, 1, dn).wait_recv()
        gout += [block(yo[1], hi, 5, dn)]
        gout[5].start()
        block(yo[3], hi, 2, up).wait_recv()
        acc[...] += dot1(pts[yo[3]], gath[it, yo[3]])
        block(yo[1], lo, 3, dn).wait_recv()
        acc[...] += dot1(pts[yo[1]], gath[it, yo[1]])
        block(yo[2], lo, 4, up).wait_recv()
        block(yo[2], hi, 5, dn).wait_recv()
        part[it, 0] = acc[oth] + dot1(pts[yo[2], oth], gath[it, yo[2]])
        pc = rdma(part.at[it, 0], part.at[it, 1], s_pt.at[it], r_pt.at[it], at(c_=other))
        pc.start()
        cross = acc[own] + dot1(pts[yo[2], own], gath[it, yo[2]])
        pc.wait_recv()
        cross += part[it, 1]

        facing_columns = facing[ZB + 1 : ZB + 2]
        facing_norms = facing[ZB : ZB + 1]
        squares_own = percol[:, 0:1]
        g = (
            squares_own * (facing_columns / facing_mass)
            + cross * (-2.0 / facing_mass)
            + facing_norms / facing_mass
        ) * (1.0 / marginal)
        grad[...] = g
        centred = g - jnp.sum(g, axis=1, keepdims=True) * (1.0 / RANK)
        largest = jnp.max(jnp.abs(centred))

        @pl.when(last)
        def _():
            @pl.when(swapped)
            def _():
                rdma(grad, fin.at[1], s_fin.at[1], r_fin.at[1], at(c_=vc, x_=xq)).start()

        tile = (1, 128)
        mx[it, 0] = jnp.full(tile, largest)
        for j in range(1, NY * NZ):
            rdma(mx.at[it, 0], mx.at[it, j], s_my.at[it], r_my.at[it],
                 at(y_=yz[j][0], z_=yz[j][1])).start()
        for cpy in [cp, up1, dn1, up2, dn2, up3, dn3, pc] + gout:
            cpy.wait_send()
        sent(stat.at[it, pl.ds(1, NY - 1)], s_st.at[it, 0])
        sent(statz.at[it, pl.ds(1, NZ - 1)], s_st.at[it, 1])
        sent(zrecv.at[it, pl.ds(1, NZ - 1)], s_z.at[it])
        sent(xall.at[it, pl.ds(0, NX - 1)], s_x.at[it])
        sent(gath.at[it, y, pl.ds(0, (NZ - 1) * ZB)], s_gz.at[it])
        arrived(mx.at[it, pl.ds(1, NY * NZ - 1)], r_my.at[it])
        mx[it, NY * NZ] = jnp.max(mx[it, : NY * NZ], axis=0)
        for j in range(1, 8):
            rdma(mx.at[it, NY * NZ], mx.at[it, NY * NZ + j], s_mc.at[it], r_mc.at[it],
                 at(c_=cx[j][0], x_=cx[j][1])).start()
        sent(mx.at[it, pl.ds(1, NY * NZ - 1)], s_my.at[it])
        arrived(mx.at[it, pl.ds(NY * NZ + 1, 7)], r_mc.at[it])
        m = jnp.max(mx[it, NY * NZ : NY * NZ + 8], axis=0)
        rate = STEP_SCALE / (m[0:1, 0:1] + 1e-6)

        @pl.when(jnp.logical_not(last))
        def _():
            lf[...] = lf[...] - rate * grad[...]

        @pl.when(last)
        def _():
            def finish(a, b):
                u = a - rate * b
                ex = jnp.exp(u - jnp.max(u, axis=1, keepdims=True))
                out[...] = ex / jnp.sum(ex, axis=1, keepdims=True)

            @pl.when(swapped)
            def _():
                for k, src in ((0, lf), (1, grad)):
                    cpy = rdma(src, fin.at[k], s_fin.at[k], r_fin.at[k], at(c_=vc, x_=xq))
                    cpy.wait_send()
                    cpy.wait_recv()
                finish(fin[0], fin[1])

            @pl.when(jnp.logical_not(swapped))
            def _():
                finish(lf[...], grad[...])

        sent(mx.at[it, pl.ds(NY * NZ + 1, 7)], s_mc.at[it])
        return 0

    lax.fori_loop(0, ITERS, step, 0)

    meta_remote.wait_send()

    @pl.when(swapped)
    def _():
        meta_own.wait_send()
        for j in range(2, NY):
            each_piece(j, wait_send)

    @pl.when(jnp.logical_not(swapped))
    def _():
        for b in order:
            half_out(b).wait_send()

    @pl.when(relays)
    def _():
        for j in range(NY):
            for r in range(2):
                forward(j, r).wait_send()


def body(points, log_factor, masses):
    mass = masses.reshape(1, ROWS)
    f32 = jnp.float32
    vm = lambda *s: pltpu.VMEM(s, f32)
    dma = lambda *s: pltpu.SemaphoreType.DMA(s)
    n = ITERS
    share = pl.pallas_call(
        kernel,
        out_shape=jax.ShapeDtypeStruct((ROWS, RANK), f32),
        in_specs=[pl.BlockSpec(memory_space=pltpu.HBM)] * 2
        + [pl.BlockSpec(memory_space=pltpu.VMEM)],
        out_specs=pl.BlockSpec(memory_space=pltpu.VMEM),
        scratch_shapes=[
            vm(NY, 2 * ROWS, YB), vm(ROWS, 2 * HALF), vm(2, NY, 128, YB), vm(ROWS, RANK),
            vm(2, 8, ROWS), vm(8, ROWS), vm(ROWS, 8),
            vm(n, 2 * ROWS, RANK), vm(n, NY, YB, RANK), vm(n, 2, 128, RANK), vm(n, 2, YB, RANK),
            vm(n, NY, 8, RANK), vm(n, NZ, 8, RANK), vm(n, NZ, ZB, RANK), vm(n, NZ, ZB, RANK),
            vm(n, NX, ZS, RANK),
            vm(n, NY, YB, RANK), vm(2 * ROWS, RANK), vm(n, 2, ROWS, RANK),
            vm(n, 40, 1, 128), vm(ROWS, RANK), vm(2, ROWS, RANK),
            pltpu.SemaphoreType.DMA, dma(2, 2, NY), dma(2, NY), dma(2, NY),
            dma(2, NY), dma(NY, 2), pltpu.SemaphoreType.DMA, pltpu.SemaphoreType.DMA,
            dma(2), dma(2), dma(n), dma(n), dma(n, 6), dma(n, 6), dma(n, 2), dma(n, 2),
            dma(n), dma(n), dma(n), dma(n), dma(n), dma(n), dma(n, 6), dma(n, 6),
            dma(n), dma(n), dma(n), dma(n), dma(n), dma(n), dma(2), dma(2),
        ],
        compiler_params=pltpu.CompilerParams(
            collective_id=0, has_side_effects=True, vmem_limit_bytes=62 << 20
        ),
        name="steps",
    )(points, log_factor, mass)
    return RANK * share


def solution(mesh):
    split = Mesh(mesh.devices.reshape(2, 2, 4, 2, 8), AXES)
    rows = ("xl", "c", "y", "xh", "z")
    return jax.shard_map(
        body,
        mesh=split,
        in_specs=(P(rows, None), P(rows, None), P(rows)),
        out_specs=P(rows, None),
        check_vma=False,
    )
```

```python
import functools

import jax
import jax.numpy as jnp
from jax import lax
from jax.experimental import pallas as pl
from jax.experimental.pallas import tpu as pltpu
from jax.sharding import Mesh
from jax.sharding import PartitionSpec as P

ITERS = 2
STEP_SCALE = 4.0
AXES = ("xl", "c", "y", "xh", "z")
NY, NZ, NX = 4, 8, 4
ROWS = 256
RANK = 256
HALF = 1024
YB = HALF // NY
ZB = YB // NZ
ZS = ZB + 8
HIGHEST = lax.Precision.HIGHEST


def dot0(a, b):
    return lax.dot_general(
        a, b, (((0,), (0,)), ((), ())), precision=HIGHEST, preferred_element_type=jnp.float32
    )


def dot1(a, b):
    return lax.dot_general(
        a, b, (((1,), (0,)), ((), ())), precision=HIGHEST, preferred_element_type=jnp.float32
    )


def kernel(
    points, lf_in, mass, out,
    pts, pv, relay, lf, meta, meta_out, percol, scaled, mom, ring1, ring2, stat, statz, zsend, zrecv, xall, gath, acc, part,
    mx, grad, fin,
    r_pv, s_rel, r_rel, s_fwd, s_pts, r_pts, s_lf, r_lf, s_meta, r_meta, s_sc, r_sc, s_r, r_r, s_st, r_st,
    s_z, r_z, s_x, r_x, s_gz, r_gz, s_gy, r_gy, s_pt, r_pt, s_mc, r_mc, s_my, r_my,
    s_fin, r_fin,
):
    xl, c, y, xh, z = (lax.axis_index(a) for a in AXES)
    x = 2 * xh + xl
    other = 1 - c
    swp = xl * ((c + xh) % 2)
    vc = (c + swp) % 2
    vxh = (xh + swp) % 2
    swapped = swp == 1

    def at(c_=None, x_=None, y_=None, z_=None):
        x_ = x if x_ is None else x_
        return (
            x_ % 2,
            c if c_ is None else c_,
            y if y_ is None else y_,
            x_ // 2,
            z if z_ is None else z_,
        )

    xq = 2 * vxh + xl
    yo = [(y + j) % NY for j in range(NY)]
    zo = [(z + j) % NZ for j in range(NZ)]
    xo = [(x + j) % NX for j in range(NX)]

    def hops(k, n):
        return min(k, n - k)

    zf = sorted(range(1, NZ), key=lambda j: -hops(j, NZ))
    xf = sorted(range(1, NX), key=lambda j: -hops(j, NX))
    cx = [(i, j) for i in range(2) for j in range(NX)]
    cx = sorted(cx, key=lambda k: -hops(k[1], NX) - 0.5 * k[0])
    cx = [(c if i == 0 else other, xo[j]) for i, j in cx]
    yz = [(i, j) for i in range(NY) for j in range(NZ)]
    yz = sorted(yz, key=lambda k: -hops(k[0], NY) - hops(k[1], NZ))
    yz = [(yo[i], zo[j]) for i, j in yz]
    own = pl.ds(pl.multiple_of(c * ROWS, ROWS), ROWS)
    oth = pl.ds(pl.multiple_of(other * ROWS, ROWS), ROWS)
    relays = x % 2 == 0

    def rdma(src, dst, ss, rs, dev):
        return pltpu.make_async_remote_copy(
            src_ref=src, dst_ref=dst, send_sem=ss, recv_sem=rs, device_id=dev,
            device_id_type=pl.DeviceIdType.MESH,
        )

    def sent(ref, sem):
        rdma(ref, ref, sem, sem, at(c_=other)).wait_send()

    def arrived(ref, sem):
        rdma(ref, ref, sem, sem, at(c_=other)).wait_recv()

    load = pltpu.make_async_copy(points, pv, r_pv)
    load.start()
    lf_remote = rdma(lf_in, lf, s_lf, r_lf, at(c_=vc, x_=xq))
    lf_local = pltpu.make_async_copy(lf_in, lf, r_lf)
    order = [yo[2], yo[1], yo[3], yo[0]]

    def cols(h, b, r, n):
        return points.at[pl.ds(r, n), pl.ds(pl.multiple_of(h * HALF + b * YB, YB), YB)]

    def half_local(b):
        return pltpu.make_async_copy(cols(c, b, 0, ROWS), pts.at[b, own], r_pts.at[b, c])

    def half_out(b):
        return rdma(cols(other, b, 0, ROWS), pts.at[b, own], s_pts.at[0, b], r_pts.at[b, c],
                    at(c_=other))

    def piece(j, h, r):
        return rdma(cols(h, order[j], r * 128, 128), relay.at[r, j], s_rel.at[h, r, j],
                    r_rel.at[r, j], at(c_=h, x_=xo[1] if r == 0 else xo[3]))

    def forward(j, r):
        to = xo[1] if r == 0 else xo[3]
        slot = (3 - to) // 2
        rows = pl.ds(pl.multiple_of(slot * ROWS + r * 128, 128), 128)
        return rdma(relay.at[r, j], pts.at[order[j], rows], s_fwd.at[r, j],
                    r_pts.at[order[j], slot], at(x_=to))

    @pl.when(jnp.logical_not(swapped))
    def _():
        lf_local.start()
        for b in order:
            half_local(b).start()

    barrier = pltpu.get_barrier_semaphore()
    peers = [at(y_=a, z_=b) for a, b in yz[:-1]] + [at(c_=a, x_=b) for a, b in cx[:-1]]
    for p in peers:
        pl.semaphore_signal(barrier, inc=1, device_id=p, device_id_type=pl.DeviceIdType.MESH)

    load.wait()
    squares = jnp.zeros((ROWS, 1), jnp.float32)
    for k in range(8):
        part_k = pv[:, k * 256 : (k + 1) * 256]
        squares += jnp.sum(part_k * part_k, axis=1, keepdims=True)
    squares_row = jnp.transpose(jnp.broadcast_to(squares, (ROWS, 128)))[:8]
    row = lax.broadcasted_iota(jnp.int32, (8, ROWS), 0)
    meta_out[...] = jnp.where(
        row == 0, squares_row, jnp.where(row == 1, 1.0, jnp.where(row == 2, mass[...], 0.0))
    )
    pl.semaphore_wait(barrier, len(peers))

    meta_remote = rdma(meta_out, meta.at[vc], s_meta.at[0], r_meta.at[vc],
                       at(c_=other, x_=xq))
    meta_own = rdma(meta_out, meta.at[vc], s_meta.at[1], r_meta.at[vc], at(c_=c, x_=xq))
    meta_local = pltpu.make_async_copy(meta_out, meta.at[vc], r_meta.at[vc])
    meta_remote.start()

    @pl.when(swapped)
    def _():
        meta_own.start()

    @pl.when(jnp.logical_not(swapped))
    def _():
        meta_local.start()

    def each_piece(j, act):
        for r in range(2):
            for h in range(2):
                act(piece(j, h, r))

    def start(cpy):
        cpy.start()

    def wait_send(cpy):
        cpy.wait_send()

    @pl.when(swapped)
    def _():
        lf_remote.start()
        each_piece(0, start)
        lf_remote.wait_send()
        each_piece(1, start)

    @pl.when(jnp.logical_not(swapped))
    def _():
        for b in order:
            half_out(b).start()

    lf_remote.wait_recv()
    for v in range(2):
        rdma(meta_out, meta.at[v], s_meta.at[0], r_meta.at[v], at(c_=other)).wait_recv()
    percol[...] = jnp.transpose(meta[c])

    def wait_points(b):
        for v in range(2):
            dst = pts.at[b, pl.ds(v * ROWS, ROWS)]
            rdma(dst, dst, s_pts.at[0, b], r_pts.at[b, v], at(c_=other)).wait_recv()

    def step(it, _):
        v = lf[...]
        e = jnp.exp(v - jnp.max(v, axis=1, keepdims=True))
        mass_own = percol[:, 2:3]
        scaled[it, own] = e / jnp.sum(e, axis=1, keepdims=True) * mass_own
        cp = rdma(scaled.at[it, own], scaled.at[it, own], s_sc.at[it], r_sc.at[it], at(c_=other))
        cp.start()
        last = it == ITERS - 1

        @pl.when(last)
        def _():
            @pl.when(swapped)
            def _():
                rdma(lf, fin.at[0], s_fin.at[0], r_fin.at[0], at(c_=vc, x_=xq)).start()

        def ready(j):
            @pl.when(it == 0)
            def _():
                @pl.when(relays)
                def _():
                    for r in range(2):
                        piece(j, c, r).wait_recv()
                        forward(j, r).start()

                if j < 2:
                    @pl.when(swapped)
                    def _():
                        each_piece(j, wait_send)
                        each_piece(j + 2, start)

                wait_points(order[j])

        def moment(j):
            ready(j)
            return dot0(pts[order[j]], scaled[it])

        lo, hi = pl.ds(0, 128), pl.ds(128, 128)
        up, dn = at(y_=yo[1]), at(y_=yo[3])
        ready(0)
        mom[it, 2] = dot0(pts[order[0], own], scaled[it, own])
        arrived(scaled.at[it, oth], r_sc.at[it])
        mom[it, 2] += dot0(pts[order[0], oth], scaled[it, oth])

        def ring(k, rows, dst, n, dev):
            cpy = rdma(mom.at[it, k, rows], dst, s_r.at[it, n], r_r.at[it, n], dev)
            cpy.start()
            return cpy

        up1 = ring(2, lo, ring1.at[it, 0], 0, up)
        dn1 = ring(2, hi, ring1.at[it, 1], 1, dn)
        mom[it, 1] = moment(1)
        up2 = ring(1, hi, ring2.at[it, 0, hi], 2, up)
        mom[it, 3] = moment(2)
        dn2 = ring(3, lo, ring2.at[it, 1, lo], 3, dn)
        stat[it, 0] = dot1(meta[0], scaled[it, :ROWS]) + dot1(meta[1], scaled[it, ROWS:])
        for j in range(1, NY):
            rdma(stat.at[it, 0], stat.at[it, j], s_st.at[it, 0], r_st.at[it, 0],
                 at(y_=yo[j])).start()
        up1.wait_recv()
        mom[it, 1, lo] += ring1[it, 0]
        up3 = ring(1, lo, ring2.at[it, 0, lo], 4, up)
        dn1.wait_recv()
        mom[it, 3, hi] += ring1[it, 1]
        dn3 = ring(3, hi, ring2.at[it, 1, hi], 5, dn)

        mom[it, 0] = moment(3)

        arrived(stat.at[it, pl.ds(1, NY - 1)], r_st.at[it, 0])
        statz[it, 0] = stat[it, 0] + stat[it, 1] + stat[it, 2] + stat[it, 3]
        for j in zf:
            rdma(statz.at[it, 0], statz.at[it, j], s_st.at[it, 1], r_st.at[it, 1],
                 at(z_=zo[j])).start()
        for cpy in (up2, dn2, up3, dn3):
            cpy.wait_recv()
        for k in range(NZ):
            r = slice(k * ZB, (k + 1) * ZB)
            zsend[it, k] = mom[it, 0, r] + ring2[it, 0, r] + ring2[it, 1, r]

        for j in zf:
            rdma(zsend.at[it, zo[j]], zrecv.at[it, j], s_z.at[it], r_z.at[it],
                 at(z_=zo[j])).start()
        arrived(zrecv.at[it, pl.ds(1, NZ - 1)], r_z.at[it])
        shard = zsend[it, z]
        for j in range(1, NZ):
            shard += zrecv[it, j]
        arrived(statz.at[it, pl.ds(1, NZ - 1)], r_st.at[it, 1])

        xall[it, x, :ZB] = shard
        xall[it, x, ZB:] = jnp.sum(statz[it], axis=0)
        for j in xf:
            rdma(xall.at[it, x], xall.at[it, x], s_x.at[it], r_x.at[it], at(x_=xo[j])).start()
        arrived(xall.at[it, pl.ds(0, NX - 1)], r_x.at[it])
        source = xall[it, 0] + xall[it, 1] + xall[it, 2]
        target = xall[it, 3]
        is_target = x == 3
        facing = jnp.where(is_target, source, target)

        zrows = pl.ds(pl.multiple_of(z * ZB, ZB), ZB)
        gath[it, y, zrows] = facing[:ZB]
        for j in zf:
            rdma(gath.at[it, y, zrows], gath.at[it, y, zrows], s_gz.at[it], r_gz.at[it],
                 at(z_=zo[j])).start()
        source_mass = jnp.sum(source[ZB + 1 : ZB + 2])
        target_mass = jnp.sum(target[ZB + 1 : ZB + 2])
        facing_mass = jnp.where(is_target, source_mass, target_mass)
        marginal = 0.5 * (source[ZB + 1 : ZB + 2] / source_mass
                          + target[ZB + 1 : ZB + 2] / target_mass)
        arrived(gath.at[it, y, pl.ds(0, (NZ - 1) * ZB)], r_gz.at[it])

        def block(b, rows, n, dev):
            ref = gath.at[it, b, rows]
            return rdma(ref, ref, s_gy.at[it, n], r_gy.at[it, n], dev)

        gout = [block(y, lo, 0, up), block(y, hi, 1, dn), block(y, hi, 2, up),
                block(y, lo, 3, dn)]
        for cpy in gout:
            cpy.start()
        acc[...] = dot1(pts[y], gath[it, y])
        block(yo[3], lo, 0, up).wait_recv()
        gout += [block(yo[3], lo, 4, up)]
        gout[4].start()
        block(yo[1], hi, 1, dn).wait_recv()
        gout += [block(yo[1], hi, 5, dn)]
        gout[5].start()
        block(yo[3], hi, 2, up).wait_recv()
        acc[...] += dot1(pts[yo[3]], gath[it, yo[3]])
        block(yo[1], lo, 3, dn).wait_recv()
        acc[...] += dot1(pts[yo[1]], gath[it, yo[1]])
        block(yo[2], lo, 4, up).wait_recv()
        block(yo[2], hi, 5, dn).wait_recv()
        part[it, 0] = acc[oth] + dot1(pts[yo[2], oth], gath[it, yo[2]])
        pc = rdma(part.at[it, 0], part.at[it, 1], s_pt.at[it], r_pt.at[it], at(c_=other))
        pc.start()
        cross = acc[own] + dot1(pts[yo[2], own], gath[it, yo[2]])
        pc.wait_recv()
        cross += part[it, 1]

        facing_columns = facing[ZB + 1 : ZB + 2]
        facing_norms = facing[ZB : ZB + 1]
        squares_own = percol[:, 0:1]
        g = (
            squares_own * (facing_columns / facing_mass)
            + cross * (-2.0 / facing_mass)
            + facing_norms / facing_mass
        ) * (1.0 / marginal)
        grad[...] = g
        centred = g - jnp.sum(g, axis=1, keepdims=True) * (1.0 / RANK)
        largest = jnp.max(jnp.abs(centred))

        @pl.when(last)
        def _():
            @pl.when(swapped)
            def _():
                rdma(grad, fin.at[1], s_fin.at[1], r_fin.at[1], at(c_=vc, x_=xq)).start()

        tile = (1, 128)
        mx[it, 0] = jnp.full(tile, largest)
        for j in range(1, NY * NZ):
            rdma(mx.at[it, 0], mx.at[it, j], s_my.at[it], r_my.at[it],
                 at(y_=yz[j - 1][0], z_=yz[j - 1][1])).start()
        for cpy in [cp, up1, dn1, up2, dn2, up3, dn3, pc] + gout:
            cpy.wait_send()
        sent(stat.at[it, pl.ds(1, NY - 1)], s_st.at[it, 0])
        sent(statz.at[it, pl.ds(1, NZ - 1)], s_st.at[it, 1])
        sent(zrecv.at[it, pl.ds(1, NZ - 1)], s_z.at[it])
        sent(xall.at[it, pl.ds(0, NX - 1)], s_x.at[it])
        sent(gath.at[it, y, pl.ds(0, (NZ - 1) * ZB)], s_gz.at[it])
        arrived(mx.at[it, pl.ds(1, NY * NZ - 1)], r_my.at[it])
        mx[it, NY * NZ] = jnp.max(mx[it, : NY * NZ], axis=0)
        for j in range(1, 8):
            rdma(mx.at[it, NY * NZ], mx.at[it, NY * NZ + j], s_mc.at[it], r_mc.at[it],
                 at(c_=cx[j - 1][0], x_=cx[j - 1][1])).start()
        sent(mx.at[it, pl.ds(1, NY * NZ - 1)], s_my.at[it])
        arrived(mx.at[it, pl.ds(NY * NZ + 1, 7)], r_mc.at[it])
        m = jnp.max(mx[it, NY * NZ : NY * NZ + 8], axis=0)
        rate = STEP_SCALE / (m[0:1, 0:1] + 1e-6)

        @pl.when(jnp.logical_not(last))
        def _():
            lf[...] = lf[...] - rate * grad[...]

        @pl.when(last)
        def _():
            def finish(a, b):
                u = a - rate * b
                ex = jnp.exp(u - jnp.max(u, axis=1, keepdims=True))
                out[...] = ex / jnp.sum(ex, axis=1, keepdims=True)

            @pl.when(swapped)
            def _():
                for k, src in ((0, lf), (1, grad)):
                    cpy = rdma(src, fin.at[k], s_fin.at[k], r_fin.at[k], at(c_=vc, x_=xq))
                    cpy.wait_send()
                    cpy.wait_recv()
                finish(fin[0], fin[1])

            @pl.when(jnp.logical_not(swapped))
            def _():
                finish(lf[...], grad[...])

        sent(mx.at[it, pl.ds(NY * NZ + 1, 7)], s_mc.at[it])
        return 0

    lax.fori_loop(0, ITERS, step, 0)

    meta_remote.wait_send()

    @pl.when(swapped)
    def _():
        meta_own.wait_send()
        for j in range(2, NY):
            each_piece(j, wait_send)

    @pl.when(jnp.logical_not(swapped))
    def _():
        for b in order:
            half_out(b).wait_send()

    @pl.when(relays)
    def _():
        for j in range(NY):
            for r in range(2):
                forward(j, r).wait_send()


def body(points, log_factor, masses):
    mass = masses.reshape(1, ROWS)
    f32 = jnp.float32
    vm = lambda *s: pltpu.VMEM(s, f32)
    dma = lambda *s: pltpu.SemaphoreType.DMA(s)
    n = ITERS
    share = pl.pallas_call(
        kernel,
        out_shape=pltpu.VMEM((ROWS, RANK), f32),
        in_specs=[pl.BlockSpec(memory_space=pltpu.HBM)] * 2
        + [pl.BlockSpec(memory_space=pltpu.VMEM)],
        out_specs=pl.BlockSpec(memory_space=pltpu.VMEM),
        scratch_shapes=[
            vm(NY, 2 * ROWS, YB), vm(ROWS, 2 * HALF), vm(2, NY, 128, YB), vm(ROWS, RANK),
            vm(2, 8, ROWS), vm(8, ROWS), vm(ROWS, 8),
            vm(n, 2 * ROWS, RANK), vm(n, NY, YB, RANK), vm(n, 2, 128, RANK), vm(n, 2, YB, RANK),
            vm(n, NY, 8, RANK), vm(n, NZ, 8, RANK), vm(n, NZ, ZB, RANK), vm(n, NZ, ZB, RANK),
            vm(n, NX, ZS, RANK),
            vm(n, NY, YB, RANK), vm(2 * ROWS, RANK), vm(n, 2, ROWS, RANK),
            vm(n, 40, 1, 128), vm(ROWS, RANK), vm(2, ROWS, RANK),
            pltpu.SemaphoreType.DMA, dma(2, 2, NY), dma(2, NY), dma(2, NY),
            dma(2, NY), dma(NY, 2), pltpu.SemaphoreType.DMA, pltpu.SemaphoreType.DMA,
            dma(2), dma(2), dma(n), dma(n), dma(n, 6), dma(n, 6), dma(n, 2), dma(n, 2),
            dma(n), dma(n), dma(n), dma(n), dma(n), dma(n), dma(n, 6), dma(n, 6),
            dma(n), dma(n), dma(n), dma(n), dma(n), dma(n), dma(2), dma(2),
        ],
        compiler_params=pltpu.CompilerParams(
            collective_id=0, has_side_effects=True, vmem_limit_bytes=62 << 20
        ),
        name="steps",
    )(points, log_factor, mass)
    return RANK * share


def solution(mesh):
    split = Mesh(mesh.devices.reshape(2, 2, 4, 2, 8), AXES)
    rows = ("xl", "c", "y", "xh", "z")
    return jax.shard_map(
        body,
        mesh=split,
        in_specs=(P(rows, None), P(rows, None), P(rows)),
        out_specs=P(rows, None),
        check_vma=False,
    )
```

```python
import functools

import jax
import jax.numpy as jnp
from jax import lax
from jax.experimental import pallas as pl
from jax.experimental.pallas import tpu as pltpu
from jax.sharding import Mesh
from jax.sharding import PartitionSpec as P

ITERS = 2
STEP_SCALE = 4.0
AXES = ("xl", "c", "y", "xh", "z")
NY, NZ, NX = 4, 8, 4
ROWS = 256
RANK = 256
HALF = 1024
YB = HALF // NY
ZB = YB // NZ
ZS = ZB + 8
ZA, ZY = ZB - 8, 8
YA = NZ * ZA
HIGHEST = lax.Precision.HIGHEST


def dot0(a, b):
    return lax.dot_general(
        a, b, (((0,), (0,)), ((), ())), precision=HIGHEST, preferred_element_type=jnp.float32
    )


def dot1(a, b):
    return lax.dot_general(
        a, b, (((1,), (0,)), ((), ())), precision=HIGHEST, preferred_element_type=jnp.float32
    )


def kernel(
    points, lf_in, mass, out,
    pts, pv, relay, lf, meta, meta_out, percol, scaled, mom, ring1, ring2, stat, statz, zsend, zrecv, xall, gath, acc, part,
    mx, grad, fin,
    r_pv, s_rel, r_rel, s_fwd, s_pts, r_pts, s_lf, r_lf, s_meta, r_meta, s_sc, r_sc, s_r, r_r, s_st, r_st,
    s_z, r_z, s_x, r_x, s_gz, r_gz, s_gb, r_gb, s_gy, r_gy, s_pt, r_pt, s_mc, r_mc, s_my, r_my,
    s_fin, r_fin,
):
    xl, c, y, xh, z = (lax.axis_index(a) for a in AXES)
    x = 2 * xh + xl
    other = 1 - c
    swp = xl * ((c + xh) % 2)
    vc = (c + swp) % 2
    vxh = (xh + swp) % 2
    swapped = swp == 1

    def at(c_=None, x_=None, y_=None, z_=None):
        x_ = x if x_ is None else x_
        return (
            x_ % 2,
            c if c_ is None else c_,
            y if y_ is None else y_,
            x_ // 2,
            z if z_ is None else z_,
        )

    xq = 2 * vxh + xl
    yo = [(y + j) % NY for j in range(NY)]
    zo = [(z + j) % NZ for j in range(NZ)]
    xo = [(x + j) % NX for j in range(NX)]

    def hops(k, n):
        return min(k, n - k)

    zf = sorted(range(1, NZ), key=lambda j: -hops(j, NZ))
    xf = sorted(range(1, NX), key=lambda j: -hops(j, NX))
    cx = [(i, j) for i in range(2) for j in range(NX)]
    cx = sorted(cx, key=lambda k: -hops(k[1], NX) - 0.5 * k[0])
    cx = [(c if i == 0 else other, xo[j]) for i, j in cx]
    yz = [(i, j) for i in range(NY) for j in range(NZ)]
    yz = sorted(yz, key=lambda k: -hops(k[0], NY) - hops(k[1], NZ))
    yz = [(yo[i], zo[j]) for i, j in yz]
    own = pl.ds(pl.multiple_of(c * ROWS, ROWS), ROWS)
    oth = pl.ds(pl.multiple_of(other * ROWS, ROWS), ROWS)
    relays = x % 2 == 0

    def rdma(src, dst, ss, rs, dev):
        return pltpu.make_async_remote_copy(
            src_ref=src, dst_ref=dst, send_sem=ss, recv_sem=rs, device_id=dev,
            device_id_type=pl.DeviceIdType.MESH,
        )

    def sent(ref, sem):
        rdma(ref, ref, sem, sem, at(c_=other)).wait_send()

    def arrived(ref, sem):
        rdma(ref, ref, sem, sem, at(c_=other)).wait_recv()

    load = pltpu.make_async_copy(points, pv, r_pv)
    load.start()
    lf_remote = rdma(lf_in, lf, s_lf, r_lf, at(c_=vc, x_=xq))
    lf_local = pltpu.make_async_copy(lf_in, lf, r_lf)
    order = [yo[2], yo[1], yo[3], yo[0]]

    def cols(h, b, r, n):
        return points.at[pl.ds(r, n), pl.ds(pl.multiple_of(h * HALF + b * YB, YB), YB)]

    def half_local(b):
        return pltpu.make_async_copy(cols(c, b, 0, ROWS), pts.at[b, own], r_pts.at[b, c])

    def half_out(b):
        return rdma(cols(other, b, 0, ROWS), pts.at[b, own], s_pts.at[0, b], r_pts.at[b, c],
                    at(c_=other))

    def piece(j, h, r):
        return rdma(cols(h, order[j], r * 128, 128), relay.at[r, j], s_rel.at[h, r, j],
                    r_rel.at[r, j], at(c_=h, x_=xo[1] if r == 0 else xo[3]))

    def forward(j, r):
        to = xo[1] if r == 0 else xo[3]
        slot = (3 - to) // 2
        rows = pl.ds(pl.multiple_of(slot * ROWS + r * 128, 128), 128)
        return rdma(relay.at[r, j], pts.at[order[j], rows], s_fwd.at[r, j],
                    r_pts.at[order[j], slot], at(x_=to))

    @pl.when(jnp.logical_not(swapped))
    def _():
        lf_local.start()
        for b in order:
            half_local(b).start()

    barrier = pltpu.get_barrier_semaphore()
    peers = [at(y_=a, z_=b) for a, b in yz[:-1]] + [at(c_=a, x_=b) for a, b in cx[:-1]]
    for p in peers:
        pl.semaphore_signal(barrier, inc=1, device_id=p, device_id_type=pl.DeviceIdType.MESH)

    load.wait()
    squares = jnp.zeros((ROWS, 1), jnp.float32)
    for k in range(8):
        part_k = pv[:, k * 256 : (k + 1) * 256]
        squares += jnp.sum(part_k * part_k, axis=1, keepdims=True)
    squares_row = jnp.transpose(jnp.broadcast_to(squares, (ROWS, 128)))[:8]
    row = lax.broadcasted_iota(jnp.int32, (8, ROWS), 0)
    meta_out[...] = jnp.where(
        row == 0, squares_row, jnp.where(row == 1, 1.0, jnp.where(row == 2, mass[...], 0.0))
    )
    pl.semaphore_wait(barrier, len(peers))

    meta_remote = rdma(meta_out, meta.at[vc], s_meta.at[0], r_meta.at[vc],
                       at(c_=other, x_=xq))
    meta_own = rdma(meta_out, meta.at[vc], s_meta.at[1], r_meta.at[vc], at(c_=c, x_=xq))
    meta_local = pltpu.make_async_copy(meta_out, meta.at[vc], r_meta.at[vc])
    meta_remote.start()

    @pl.when(swapped)
    def _():
        meta_own.start()

    @pl.when(jnp.logical_not(swapped))
    def _():
        meta_local.start()

    def each_piece(j, act):
        for r in range(2):
            for h in range(2):
                act(piece(j, h, r))

    def start(cpy):
        cpy.start()

    def wait_send(cpy):
        cpy.wait_send()

    @pl.when(swapped)
    def _():
        lf_remote.start()
        each_piece(0, start)
        lf_remote.wait_send()
        each_piece(1, start)

    @pl.when(jnp.logical_not(swapped))
    def _():
        for b in order:
            half_out(b).start()

    lf_remote.wait_recv()
    for v in range(2):
        rdma(meta_out, meta.at[v], s_meta.at[0], r_meta.at[v], at(c_=other)).wait_recv()
    percol[...] = jnp.transpose(meta[c])

    def wait_points(b):
        for v in range(2):
            dst = pts.at[b, pl.ds(v * ROWS, ROWS)]
            rdma(dst, dst, s_pts.at[0, b], r_pts.at[b, v], at(c_=other)).wait_recv()

    def step(it, _):
        v = lf[...]
        e = jnp.exp(v - jnp.max(v, axis=1, keepdims=True))
        mass_own = percol[:, 2:3]
        scaled[it, own] = e / jnp.sum(e, axis=1, keepdims=True) * mass_own
        cp = rdma(scaled.at[it, own], scaled.at[it, own], s_sc.at[it], r_sc.at[it], at(c_=other))
        cp.start()
        last = it == ITERS - 1

        @pl.when(last)
        def _():
            @pl.when(swapped)
            def _():
                rdma(lf, fin.at[0], s_fin.at[0], r_fin.at[0], at(c_=vc, x_=xq)).start()

        def ready(j):
            @pl.when(it == 0)
            def _():
                @pl.when(relays)
                def _():
                    for r in range(2):
                        piece(j, c, r).wait_recv()
                        forward(j, r).start()

                if j < 2:
                    @pl.when(swapped)
                    def _():
                        each_piece(j, wait_send)
                        each_piece(j + 2, start)

                wait_points(order[j])

        def moment(j):
            ready(j)
            return dot0(pts[order[j]], scaled[it])

        lo, hi = pl.ds(0, 128), pl.ds(128, 128)
        up, dn = at(y_=yo[1]), at(y_=yo[3])
        ready(0)
        mom[it, 2] = dot0(pts[order[0], own], scaled[it, own])
        arrived(scaled.at[it, oth], r_sc.at[it])
        mom[it, 2] += dot0(pts[order[0], oth], scaled[it, oth])

        def ring(k, rows, dst, n, dev):
            cpy = rdma(mom.at[it, k, rows], dst, s_r.at[it, n], r_r.at[it, n], dev)
            cpy.start()
            return cpy

        up1 = ring(2, lo, ring1.at[it, 0], 0, up)
        dn1 = ring(2, hi, ring1.at[it, 1], 1, dn)
        mom[it, 1] = moment(1)
        up2 = ring(1, hi, ring2.at[it, 0, hi], 2, up)
        mom[it, 3] = moment(2)
        dn2 = ring(3, lo, ring2.at[it, 1, lo], 3, dn)
        stat[it, 0] = dot1(meta[0], scaled[it, :ROWS]) + dot1(meta[1], scaled[it, ROWS:])
        for j in range(1, NY):
            rdma(stat.at[it, 0], stat.at[it, j], s_st.at[it, 0], r_st.at[it, 0],
                 at(y_=yo[j])).start()
        up1.wait_recv()
        mom[it, 1, lo] += ring1[it, 0]
        up3 = ring(1, lo, ring2.at[it, 0, lo], 4, up)
        dn1.wait_recv()
        mom[it, 3, hi] += ring1[it, 1]
        dn3 = ring(3, hi, ring2.at[it, 1, hi], 5, dn)

        mom[it, 0] = moment(3)

        arrived(stat.at[it, pl.ds(1, NY - 1)], r_st.at[it, 0])
        statz[it, 0] = stat[it, 0] + stat[it, 1] + stat[it, 2] + stat[it, 3]
        for j in zf:
            rdma(statz.at[it, 0], statz.at[it, j], s_st.at[it, 1], r_st.at[it, 1],
                 at(z_=zo[j])).start()
        for cpy in (up2, dn2, up3, dn3):
            cpy.wait_recv()

        def fill(k):
            for dst, n, first in ((0, ZA, k * ZA), (ZA, ZY, YA + k * ZY)):
                r = pl.ds(pl.multiple_of(first, 8), n)
                zsend[it, k, dst : dst + n] = mom[it, 0, r] + ring2[it, 0, r] + ring2[it, 1, r]

        for j in zf:
            fill(zo[j])
            rdma(zsend.at[it, zo[j]], zrecv.at[it, j], s_z.at[it], r_z.at[it],
                 at(z_=zo[j])).start()
        fill(z)
        arrived(zrecv.at[it, pl.ds(1, NZ - 1)], r_z.at[it])
        shard = zsend[it, z]
        for j in range(1, NZ):
            shard += zrecv[it, j]
        arrived(statz.at[it, pl.ds(1, NZ - 1)], r_st.at[it, 1])

        xall[it, x, :ZB] = shard
        xall[it, x, ZB:] = jnp.sum(statz[it], axis=0)
        for j in xf:
            rdma(xall.at[it, x], xall.at[it, x], s_x.at[it], r_x.at[it], at(x_=xo[j])).start()
        arrived(xall.at[it, pl.ds(0, NX - 1)], r_x.at[it])
        source = xall[it, 0] + xall[it, 1] + xall[it, 2]
        target = xall[it, 3]
        is_target = x == 3
        facing = jnp.where(is_target, source, target)

        zrows = pl.ds(pl.multiple_of(z * ZA, 8), ZA)
        yrows = pl.ds(pl.multiple_of(YA + z * ZY, 8), ZY)
        gath[it, y, zrows] = facing[:ZA]
        gath[it, y, yrows] = facing[ZA:ZB]
        for j in (2, 1, 3):
            rdma(gath.at[it, y, yrows], gath.at[it, y, yrows], s_gb.at[it, 0], r_gb.at[it, 0],
                 at(y_=yo[j])).start()
        for j in zf:
            rdma(gath.at[it, y, zrows], gath.at[it, y, zrows], s_gz.at[it], r_gz.at[it],
                 at(z_=zo[j])).start()
        source_mass = jnp.sum(source[ZB + 1 : ZB + 2])
        target_mass = jnp.sum(target[ZB + 1 : ZB + 2])
        facing_mass = jnp.where(is_target, source_mass, target_mass)
        marginal = 0.5 * (source[ZB + 1 : ZB + 2] / source_mass
                          + target[ZB + 1 : ZB + 2] / target_mass)
        arrived(gath.at[it, pl.ds(0, NY - 1), yrows], r_gb.at[it, 0])
        every = gath.at[it, pl.ds(0, NY), yrows]
        for j in zf:
            rdma(every, every, s_gb.at[it, 1], r_gb.at[it, 1], at(z_=zo[j])).start()
        arrived(gath.at[it, y, pl.ds(0, (NZ - 1) * ZA)], r_gz.at[it])
        glo, ghi = pl.ds(0, YA // 2), pl.ds(YA // 2, YA // 2)

        def block(b, rows, n, dev):
            ref = gath.at[it, b, rows]
            return rdma(ref, ref, s_gy.at[it, n], r_gy.at[it, n], dev)

        gout = [block(y, glo, 0, up), block(y, ghi, 1, dn), block(y, ghi, 2, up),
                block(y, glo, 3, dn)]
        for cpy in gout:
            cpy.start()
        block(yo[3], glo, 0, up).wait_recv()
        gout += [block(yo[3], glo, 4, up)]
        gout[4].start()
        block(yo[1], ghi, 1, dn).wait_recv()
        gout += [block(yo[1], ghi, 5, dn)]
        gout[5].start()
        arrived(gath.at[it, 0, pl.ds(0, (NZ - 1) * NY * ZY)], r_gb.at[it, 1])
        acc[...] = dot1(pts[y], gath[it, y])
        block(yo[3], ghi, 2, up).wait_recv()
        acc[...] += dot1(pts[yo[3]], gath[it, yo[3]])
        block(yo[1], glo, 3, dn).wait_recv()
        acc[...] += dot1(pts[yo[1]], gath[it, yo[1]])
        block(yo[2], glo, 4, up).wait_recv()
        block(yo[2], ghi, 5, dn).wait_recv()
        part[it, 0] = acc[oth] + dot1(pts[yo[2], oth], gath[it, yo[2]])
        pc = rdma(part.at[it, 0], part.at[it, 1], s_pt.at[it], r_pt.at[it], at(c_=other))
        pc.start()
        cross = acc[own] + dot1(pts[yo[2], own], gath[it, yo[2]])
        pc.wait_recv()
        cross += part[it, 1]

        facing_columns = facing[ZB + 1 : ZB + 2]
        facing_norms = facing[ZB : ZB + 1]
        squares_own = percol[:, 0:1]
        g = (
            squares_own * (facing_columns / facing_mass)
            + cross * (-2.0 / facing_mass)
            + facing_norms / facing_mass
        ) * (1.0 / marginal)
        grad[...] = g
        centred = g - jnp.sum(g, axis=1, keepdims=True) * (1.0 / RANK)
        largest = jnp.max(jnp.abs(centred))

        @pl.when(last)
        def _():
            @pl.when(swapped)
            def _():
                rdma(grad, fin.at[1], s_fin.at[1], r_fin.at[1], at(c_=vc, x_=xq)).start()

        tile = (1, 128)
        mx[it, 0] = jnp.full(tile, largest)
        for j in range(1, NY * NZ):
            rdma(mx.at[it, 0], mx.at[it, j], s_my.at[it], r_my.at[it],
                 at(y_=yz[j - 1][0], z_=yz[j - 1][1])).start()
        for cpy in [cp, up1, dn1, up2, dn2, up3, dn3, pc] + gout:
            cpy.wait_send()
        sent(stat.at[it, pl.ds(1, NY - 1)], s_st.at[it, 0])
        sent(statz.at[it, pl.ds(1, NZ - 1)], s_st.at[it, 1])
        sent(zrecv.at[it, pl.ds(1, NZ - 1)], s_z.at[it])
        sent(xall.at[it, pl.ds(0, NX - 1)], s_x.at[it])
        sent(gath.at[it, y, pl.ds(0, (NZ - 1) * ZA)], s_gz.at[it])
        sent(gath.at[it, pl.ds(0, NY - 1), yrows], s_gb.at[it, 0])
        sent(gath.at[it, 0, pl.ds(0, (NZ - 1) * NY * ZY)], s_gb.at[it, 1])
        arrived(mx.at[it, pl.ds(1, NY * NZ - 1)], r_my.at[it])
        mx[it, NY * NZ] = jnp.max(mx[it, : NY * NZ], axis=0)
        for j in range(1, 8):
            rdma(mx.at[it, NY * NZ], mx.at[it, NY * NZ + j], s_mc.at[it], r_mc.at[it],
                 at(c_=cx[j - 1][0], x_=cx[j - 1][1])).start()
        sent(mx.at[it, pl.ds(1, NY * NZ - 1)], s_my.at[it])
        arrived(mx.at[it, pl.ds(NY * NZ + 1, 7)], r_mc.at[it])
        m = jnp.max(mx[it, NY * NZ : NY * NZ + 8], axis=0)
        rate = STEP_SCALE / (m[0:1, 0:1] + 1e-6)

        @pl.when(jnp.logical_not(last))
        def _():
            lf[...] = lf[...] - rate * grad[...]

        @pl.when(last)
        def _():
            def finish(a, b):
                u = a - rate * b
                ex = jnp.exp(u - jnp.max(u, axis=1, keepdims=True))
                out[...] = ex / jnp.sum(ex, axis=1, keepdims=True)

            @pl.when(swapped)
            def _():
                for k, src in ((0, lf), (1, grad)):
                    cpy = rdma(src, fin.at[k], s_fin.at[k], r_fin.at[k], at(c_=vc, x_=xq))
                    cpy.wait_send()
                    cpy.wait_recv()
                finish(fin[0], fin[1])

            @pl.when(jnp.logical_not(swapped))
            def _():
                finish(lf[...], grad[...])

        sent(mx.at[it, pl.ds(NY * NZ + 1, 7)], s_mc.at[it])
        return 0

    lax.fori_loop(0, ITERS, step, 0)

    meta_remote.wait_send()

    @pl.when(swapped)
    def _():
        meta_own.wait_send()
        for j in range(2, NY):
            each_piece(j, wait_send)

    @pl.when(jnp.logical_not(swapped))
    def _():
        for b in order:
            half_out(b).wait_send()

    @pl.when(relays)
    def _():
        for j in range(NY):
            for r in range(2):
                forward(j, r).wait_send()


def body(points, log_factor, masses):
    mass = masses.reshape(1, ROWS)
    f32 = jnp.float32
    vm = lambda *s: pltpu.VMEM(s, f32)
    dma = lambda *s: pltpu.SemaphoreType.DMA(s)
    n = ITERS
    share = pl.pallas_call(
        kernel,
        out_shape=pltpu.VMEM((ROWS, RANK), f32),
        in_specs=[pl.BlockSpec(memory_space=pltpu.HBM)] * 2
        + [pl.BlockSpec(memory_space=pltpu.VMEM)],
        out_specs=pl.BlockSpec(memory_space=pltpu.VMEM),
        scratch_shapes=[
            vm(NY, 2 * ROWS, YB), vm(ROWS, 2 * HALF), vm(2, NY, 128, YB), vm(ROWS, RANK),
            vm(2, 8, ROWS), vm(8, ROWS), vm(ROWS, 8),
            vm(n, 2 * ROWS, RANK), vm(n, NY, YB, RANK), vm(n, 2, 128, RANK), vm(n, 2, YB, RANK),
            vm(n, NY, 8, RANK), vm(n, NZ, 8, RANK), vm(n, NZ, ZB, RANK), vm(n, NZ, ZB, RANK),
            vm(n, NX, ZS, RANK),
            vm(n, NY, YB, RANK), vm(2 * ROWS, RANK), vm(n, 2, ROWS, RANK),
            vm(n, 40, 1, 128), vm(ROWS, RANK), vm(2, ROWS, RANK),
            pltpu.SemaphoreType.DMA, dma(2, 2, NY), dma(2, NY), dma(2, NY),
            dma(2, NY), dma(NY, 2), pltpu.SemaphoreType.DMA, pltpu.SemaphoreType.DMA,
            dma(2), dma(2), dma(n), dma(n), dma(n, 6), dma(n, 6), dma(n, 2), dma(n, 2),
            dma(n), dma(n), dma(n), dma(n), dma(n), dma(n), dma(n, 2), dma(n, 2), dma(n, 6), dma(n, 6),
            dma(n), dma(n), dma(n), dma(n), dma(n), dma(n), dma(2), dma(2),
        ],
        compiler_params=pltpu.CompilerParams(
            collective_id=0, has_side_effects=True, vmem_limit_bytes=62 << 20
        ),
        name="steps",
    )(points, log_factor, mass)
    return RANK * share


def solution(mesh):
    split = Mesh(mesh.devices.reshape(2, 2, 4, 2, 8), AXES)
    rows = ("xl", "c", "y", "xh", "z")
    return jax.shard_map(
        body,
        mesh=split,
        in_specs=(P(rows, None), P(rows, None), P(rows)),
        out_specs=P(rows, None),
        check_vma=False,
    )
```

```python
import functools

import jax
import jax.numpy as jnp
from jax import lax
from jax.experimental import pallas as pl
from jax.experimental.pallas import tpu as pltpu
from jax.sharding import Mesh
from jax.sharding import PartitionSpec as P

ITERS = 2
STEP_SCALE = 4.0
AXES = ("xl", "c", "y", "xh", "z")
NY, NZ, NX = 4, 8, 4
ROWS = 256
RANK = 256
HALF = 1024
YB = HALF // NY
ZB = YB // NZ
ZS = ZB + 8
ZA, ZY = ZB - 8, 8
YA = NZ * ZA
HIGHEST = lax.Precision.HIGHEST


def dot0(a, b):
    return lax.dot_general(
        a, b, (((0,), (0,)), ((), ())), precision=HIGHEST, preferred_element_type=jnp.float32
    )


def dot1(a, b):
    return lax.dot_general(
        a, b, (((1,), (0,)), ((), ())), precision=HIGHEST, preferred_element_type=jnp.float32
    )


def kernel(
    points, lf_in, mass, out,
    pts, pv, relay, lf, meta, meta_out, percol, scaled, mom, ring1, ring2, stat, statz, zsend, zrecv, xall, gath, acc, part,
    mx, grad, fin,
    r_pv, s_rel, r_rel, s_fwd, s_pts, r_pts, s_lf, r_lf, s_meta, r_meta, s_sc, r_sc, s_r, r_r, s_st, r_st,
    s_z, r_z, s_x, r_x, s_gz, r_gz, s_gb, r_gb, s_gy, r_gy, s_pt, r_pt, s_mc, r_mc, s_my, r_my,
    s_fin, r_fin,
):
    xl, c, y, xh, z = (lax.axis_index(a) for a in AXES)
    x = 2 * xh + xl
    other = 1 - c
    swp = xl * ((c + xh) % 2)
    vc = (c + swp) % 2
    vxh = (xh + swp) % 2
    swapped = swp == 1

    def at(c_=None, x_=None, y_=None, z_=None):
        x_ = x if x_ is None else x_
        return (
            x_ % 2,
            c if c_ is None else c_,
            y if y_ is None else y_,
            x_ // 2,
            z if z_ is None else z_,
        )

    xq = 2 * vxh + xl
    yo = [(y + j) % NY for j in range(NY)]
    zo = [(z + j) % NZ for j in range(NZ)]
    xo = [(x + j) % NX for j in range(NX)]

    def hops(k, n):
        return min(k, n - k)

    zf = sorted(range(1, NZ), key=lambda j: -hops(j, NZ))
    xf = sorted(range(1, NX), key=lambda j: -hops(j, NX))
    cz = [(i, j) for i in range(2) for j in range(NZ)]
    cz = sorted(cz, key=lambda k: -hops(k[1], NZ) - 0.5 * k[0])
    cz = [(c if i == 0 else other, zo[j]) for i, j in cz]
    xy = [(i, j) for i in range(NX) for j in range(NY)]
    xy = sorted(xy, key=lambda k: -hops(k[0], NX) - hops(k[1], NY))
    xy = [(xo[i], yo[j]) for i, j in xy]
    own = pl.ds(pl.multiple_of(c * ROWS, ROWS), ROWS)
    oth = pl.ds(pl.multiple_of(other * ROWS, ROWS), ROWS)
    relays = x % 2 == 0

    def rdma(src, dst, ss, rs, dev):
        return pltpu.make_async_remote_copy(
            src_ref=src, dst_ref=dst, send_sem=ss, recv_sem=rs, device_id=dev,
            device_id_type=pl.DeviceIdType.MESH,
        )

    def sent(ref, sem):
        rdma(ref, ref, sem, sem, at(c_=other)).wait_send()

    def arrived(ref, sem):
        rdma(ref, ref, sem, sem, at(c_=other)).wait_recv()

    load = pltpu.make_async_copy(points, pv, r_pv)
    load.start()
    lf_remote = rdma(lf_in, lf, s_lf, r_lf, at(c_=vc, x_=xq))
    lf_local = pltpu.make_async_copy(lf_in, lf, r_lf)
    order = [yo[2], yo[1], yo[3], yo[0]]

    def cols(h, b, r, n):
        return points.at[pl.ds(r, n), pl.ds(pl.multiple_of(h * HALF + b * YB, YB), YB)]

    def half_local(b):
        return pltpu.make_async_copy(cols(c, b, 0, ROWS), pts.at[b, own], r_pts.at[b, c])

    def half_out(b):
        return rdma(cols(other, b, 0, ROWS), pts.at[b, own], s_pts.at[0, b], r_pts.at[b, c],
                    at(c_=other))

    def piece(j, h, r):
        return rdma(cols(h, order[j], r * 128, 128), relay.at[r, j], s_rel.at[h, r, j],
                    r_rel.at[r, j], at(c_=h, x_=xo[1] if r == 0 else xo[3]))

    def forward(j, r):
        to = xo[1] if r == 0 else xo[3]
        slot = (3 - to) // 2
        rows = pl.ds(pl.multiple_of(slot * ROWS + r * 128, 128), 128)
        return rdma(relay.at[r, j], pts.at[order[j], rows], s_fwd.at[r, j],
                    r_pts.at[order[j], slot], at(x_=to))

    @pl.when(jnp.logical_not(swapped))
    def _():
        lf_local.start()
        for b in order:
            half_local(b).start()

    barrier = pltpu.get_barrier_semaphore()
    peers = [at(c_=a, z_=b) for a, b in cz[:-1]] + [at(x_=a, y_=b) for a, b in xy[:-1]]
    peers += [at(c_=other, x_=b) for b in xo[1:]]
    for p in peers:
        pl.semaphore_signal(barrier, inc=1, device_id=p, device_id_type=pl.DeviceIdType.MESH)

    load.wait()
    squares = jnp.zeros((ROWS, 1), jnp.float32)
    for k in range(8):
        part_k = pv[:, k * 256 : (k + 1) * 256]
        squares += jnp.sum(part_k * part_k, axis=1, keepdims=True)
    squares_row = jnp.transpose(jnp.broadcast_to(squares, (ROWS, 128)))[:8]
    row = lax.broadcasted_iota(jnp.int32, (8, ROWS), 0)
    meta_out[...] = jnp.where(
        row == 0, squares_row, jnp.where(row == 1, 1.0, jnp.where(row == 2, mass[...], 0.0))
    )
    pl.semaphore_wait(barrier, len(peers))

    meta_remote = rdma(meta_out, meta.at[vc], s_meta.at[0], r_meta.at[vc],
                       at(c_=other, x_=xq))
    meta_own = rdma(meta_out, meta.at[vc], s_meta.at[1], r_meta.at[vc], at(c_=c, x_=xq))
    meta_local = pltpu.make_async_copy(meta_out, meta.at[vc], r_meta.at[vc])
    meta_remote.start()

    @pl.when(swapped)
    def _():
        meta_own.start()

    @pl.when(jnp.logical_not(swapped))
    def _():
        meta_local.start()

    def each_piece(j, act):
        for r in range(2):
            for h in range(2):
                act(piece(j, h, r))

    def start(cpy):
        cpy.start()

    def wait_send(cpy):
        cpy.wait_send()

    @pl.when(swapped)
    def _():
        lf_remote.start()
        each_piece(0, start)
        lf_remote.wait_send()
        each_piece(1, start)

    @pl.when(jnp.logical_not(swapped))
    def _():
        for b in order:
            half_out(b).start()

    lf_remote.wait_recv()
    for v in range(2):
        rdma(meta_out, meta.at[v], s_meta.at[0], r_meta.at[v], at(c_=other)).wait_recv()
    percol[...] = jnp.transpose(meta[c])

    def wait_points(b):
        for v in range(2):
            dst = pts.at[b, pl.ds(v * ROWS, ROWS)]
            rdma(dst, dst, s_pts.at[0, b], r_pts.at[b, v], at(c_=other)).wait_recv()

    def step(it, _):
        for k in range(2):
            half = slice(k * 128, (k + 1) * 128)
            v = lf[half]
            e = jnp.exp(v - jnp.max(v, axis=1, keepdims=True))
            rows = pl.ds(pl.multiple_of(c * ROWS + k * 128, 128), 128)
            scaled[it, rows] = e / jnp.sum(e, axis=1, keepdims=True) * percol[half, 2:3]
            rdma(scaled.at[it, rows], scaled.at[it, rows], s_sc.at[it], r_sc.at[it],
                 at(c_=other)).start()
        last = it == ITERS - 1

        @pl.when(last)
        def _():
            @pl.when(swapped)
            def _():
                rdma(lf, fin.at[0], s_fin.at[0], r_fin.at[0], at(c_=vc, x_=xq)).start()

        def ready(j):
            @pl.when(it == 0)
            def _():
                @pl.when(relays)
                def _():
                    for r in range(2):
                        piece(j, c, r).wait_recv()
                        forward(j, r).start()

                if j < 2:
                    @pl.when(swapped)
                    def _():
                        each_piece(j, wait_send)
                        each_piece(j + 2, start)

                wait_points(order[j])

        def moment(j):
            ready(j)
            return dot0(pts[order[j]], scaled[it])

        lo, hi = pl.ds(0, 128), pl.ds(128, 128)
        up, dn = at(y_=yo[1]), at(y_=yo[3])
        ready(0)
        mom[it, 2] = dot0(pts[order[0], own], scaled[it, own])
        arrived(scaled.at[it, oth], r_sc.at[it])
        mom[it, 2] += dot0(pts[order[0], oth], scaled[it, oth])

        def ring(k, rows, dst, n, dev):
            cpy = rdma(mom.at[it, k, rows], dst, s_r.at[it, n], r_r.at[it, n], dev)
            cpy.start()
            return cpy

        up1 = ring(2, lo, ring1.at[it, 0], 0, up)
        dn1 = ring(2, hi, ring1.at[it, 1], 1, dn)
        mom[it, 1] = moment(1)
        up2 = ring(1, hi, ring2.at[it, 0, hi], 2, up)
        mom[it, 3] = moment(2)
        dn2 = ring(3, lo, ring2.at[it, 1, lo], 3, dn)
        stat[it, 0] = dot1(meta[0], scaled[it, :ROWS]) + dot1(meta[1], scaled[it, ROWS:])
        for j in range(1, NY):
            rdma(stat.at[it, 0], stat.at[it, j], s_st.at[it, 0], r_st.at[it, 0],
                 at(y_=yo[j])).start()
        up1.wait_recv()
        mom[it, 1, lo] += ring1[it, 0]
        up3 = ring(1, lo, ring2.at[it, 0, lo], 4, up)
        dn1.wait_recv()
        mom[it, 3, hi] += ring1[it, 1]
        dn3 = ring(3, hi, ring2.at[it, 1, hi], 5, dn)

        mom[it, 0] = moment(3)

        arrived(stat.at[it, pl.ds(1, NY - 1)], r_st.at[it, 0])
        statz[it, 0] = stat[it, 0] + stat[it, 1] + stat[it, 2] + stat[it, 3]
        for j in zf:
            rdma(statz.at[it, 0], statz.at[it, j], s_st.at[it, 1], r_st.at[it, 1],
                 at(z_=zo[j])).start()
        for cpy in (up2, dn2, up3, dn3):
            cpy.wait_recv()

        def fill(k):
            for dst, n, first in ((0, ZA, k * ZA), (ZA, ZY, YA + k * ZY)):
                r = pl.ds(pl.multiple_of(first, 8), n)
                zsend[it, k, dst : dst + n] = mom[it, 0, r] + ring2[it, 0, r] + ring2[it, 1, r]

        for j in zf:
            fill(zo[j])
            rdma(zsend.at[it, zo[j]], zrecv.at[it, j], s_z.at[it], r_z.at[it],
                 at(z_=zo[j])).start()
        fill(z)
        arrived(zrecv.at[it, pl.ds(1, NZ - 1)], r_z.at[it])
        shard = zsend[it, z]
        for j in range(1, NZ):
            shard += zrecv[it, j]
        arrived(statz.at[it, pl.ds(1, NZ - 1)], r_st.at[it, 1])

        xall[it, x, :ZB] = shard
        xall[it, x, ZB:] = jnp.sum(statz[it], axis=0)
        for j in xf:
            rdma(xall.at[it, x], xall.at[it, x], s_x.at[it], r_x.at[it], at(x_=xo[j])).start()
        arrived(xall.at[it, pl.ds(0, NX - 1)], r_x.at[it])
        source = xall[it, 0] + xall[it, 1] + xall[it, 2]
        target = xall[it, 3]
        is_target = x == 3
        facing = jnp.where(is_target, source, target)

        zrows = pl.ds(pl.multiple_of(z * ZA, 8), ZA)
        yrows = pl.ds(pl.multiple_of(YA + z * ZY, 8), ZY)
        gath[it, y, zrows] = facing[:ZA]
        gath[it, y, yrows] = facing[ZA:ZB]
        for j in (2, 1, 3):
            rdma(gath.at[it, y, yrows], gath.at[it, y, yrows], s_gb.at[it, 0], r_gb.at[it, 0],
                 at(y_=yo[j])).start()
        for j in zf:
            rdma(gath.at[it, y, zrows], gath.at[it, y, zrows], s_gz.at[it], r_gz.at[it],
                 at(z_=zo[j])).start()
        source_mass = jnp.sum(source[ZB + 1 : ZB + 2])
        target_mass = jnp.sum(target[ZB + 1 : ZB + 2])
        facing_mass = jnp.where(is_target, source_mass, target_mass)
        marginal = 0.5 * (source[ZB + 1 : ZB + 2] / source_mass
                          + target[ZB + 1 : ZB + 2] / target_mass)
        arrived(gath.at[it, pl.ds(0, NY - 1), yrows], r_gb.at[it, 0])
        every = gath.at[it, pl.ds(0, NY), yrows]
        for j in zf:
            rdma(every, every, s_gb.at[it, 1], r_gb.at[it, 1], at(z_=zo[j])).start()
        arrived(gath.at[it, y, pl.ds(0, (NZ - 1) * ZA)], r_gz.at[it])
        glo, ghi = pl.ds(0, YA // 2), pl.ds(YA // 2, YA // 2)

        def block(b, rows, n, dev):
            ref = gath.at[it, b, rows]
            return rdma(ref, ref, s_gy.at[it, n], r_gy.at[it, n], dev)

        gout = [block(y, glo, 0, up), block(y, ghi, 1, dn), block(y, ghi, 2, up),
                block(y, glo, 3, dn)]
        for cpy in gout:
            cpy.start()
        block(yo[3], glo, 0, up).wait_recv()
        gout += [block(yo[3], glo, 4, up)]
        gout[4].start()
        block(yo[1], ghi, 1, dn).wait_recv()
        gout += [block(yo[1], ghi, 5, dn)]
        gout[5].start()
        arrived(gath.at[it, 0, pl.ds(0, (NZ - 1) * NY * ZY)], r_gb.at[it, 1])
        acc[...] = dot1(pts[y], gath[it, y])
        block(yo[3], ghi, 2, up).wait_recv()
        acc[...] += dot1(pts[yo[3]], gath[it, yo[3]])
        block(yo[1], glo, 3, dn).wait_recv()
        acc[...] += dot1(pts[yo[1]], gath[it, yo[1]])
        block(yo[2], glo, 4, up).wait_recv()
        block(yo[2], ghi, 5, dn).wait_recv()
        part[it, 0] = acc[oth] + dot1(pts[yo[2], oth], gath[it, yo[2]])
        pc = rdma(part.at[it, 0], part.at[it, 1], s_pt.at[it], r_pt.at[it], at(c_=other))
        pc.start()
        cross = acc[own] + dot1(pts[yo[2], own], gath[it, yo[2]])
        pc.wait_recv()
        cross += part[it, 1]

        facing_columns = facing[ZB + 1 : ZB + 2]
        facing_norms = facing[ZB : ZB + 1]
        squares_own = percol[:, 0:1]
        g = (
            squares_own * (facing_columns / facing_mass)
            + cross * (-2.0 / facing_mass)
            + facing_norms / facing_mass
        ) * (1.0 / marginal)
        grad[...] = g
        centred = g - jnp.sum(g, axis=1, keepdims=True) * (1.0 / RANK)
        largest = jnp.max(jnp.abs(centred))

        @pl.when(last)
        def _():
            @pl.when(swapped)
            def _():
                rdma(grad, fin.at[1], s_fin.at[1], r_fin.at[1], at(c_=vc, x_=xq)).start()

        tile = (1, 128)
        mx[it, 0] = jnp.full(tile, largest)
        for j in range(1, 16):
            rdma(mx.at[it, 0], mx.at[it, j], s_mc.at[it], r_mc.at[it],
                 at(c_=cz[j - 1][0], z_=cz[j - 1][1])).start()
        for cpy in [up1, dn1, up2, dn2, up3, dn3, pc] + gout:
            cpy.wait_send()
        sent(scaled.at[it, own], s_sc.at[it])
        sent(stat.at[it, pl.ds(1, NY - 1)], s_st.at[it, 0])
        sent(statz.at[it, pl.ds(1, NZ - 1)], s_st.at[it, 1])
        sent(zrecv.at[it, pl.ds(1, NZ - 1)], s_z.at[it])
        sent(xall.at[it, pl.ds(0, NX - 1)], s_x.at[it])
        sent(gath.at[it, y, pl.ds(0, (NZ - 1) * ZA)], s_gz.at[it])
        sent(gath.at[it, pl.ds(0, NY - 1), yrows], s_gb.at[it, 0])
        sent(gath.at[it, 0, pl.ds(0, (NZ - 1) * NY * ZY)], s_gb.at[it, 1])
        arrived(mx.at[it, pl.ds(1, 15)], r_mc.at[it])
        mx[it, 16] = jnp.max(mx[it, :16], axis=0)
        for j in range(1, 16):
            rdma(mx.at[it, 16], mx.at[it, 16 + j], s_my.at[it], r_my.at[it],
                 at(x_=xy[j - 1][0], y_=xy[j - 1][1])).start()
        sent(mx.at[it, pl.ds(1, 15)], s_mc.at[it])
        arrived(mx.at[it, pl.ds(17, 15)], r_my.at[it])
        m = jnp.max(mx[it, 16:32], axis=0)
        rate = STEP_SCALE / (m[0:1, 0:1] + 1e-6)

        @pl.when(jnp.logical_not(last))
        def _():
            lf[...] = lf[...] - rate * grad[...]

        @pl.when(last)
        def _():
            def finish(a, b):
                u = a - rate * b
                ex = jnp.exp(u - jnp.max(u, axis=1, keepdims=True))
                out[...] = ex / jnp.sum(ex, axis=1, keepdims=True)

            @pl.when(swapped)
            def _():
                for k, src in ((0, lf), (1, grad)):
                    cpy = rdma(src, fin.at[k], s_fin.at[k], r_fin.at[k], at(c_=vc, x_=xq))
                    cpy.wait_send()
                    cpy.wait_recv()
                finish(fin[0], fin[1])

            @pl.when(jnp.logical_not(swapped))
            def _():
                finish(lf[...], grad[...])

        sent(mx.at[it, pl.ds(17, 15)], s_my.at[it])
        return 0

    lax.fori_loop(0, ITERS, step, 0)

    meta_remote.wait_send()

    @pl.when(swapped)
    def _():
        meta_own.wait_send()
        for j in range(2, NY):
            each_piece(j, wait_send)

    @pl.when(jnp.logical_not(swapped))
    def _():
        for b in order:
            half_out(b).wait_send()

    @pl.when(relays)
    def _():
        for j in range(NY):
            for r in range(2):
                forward(j, r).wait_send()


def body(points, log_factor, masses):
    mass = masses.reshape(1, ROWS)
    f32 = jnp.float32
    vm = lambda *s: pltpu.VMEM(s, f32)
    dma = lambda *s: pltpu.SemaphoreType.DMA(s)
    n = ITERS
    share = pl.pallas_call(
        kernel,
        out_shape=pltpu.VMEM((ROWS, RANK), f32),
        in_specs=[pl.BlockSpec(memory_space=pltpu.HBM)] * 2
        + [pl.BlockSpec(memory_space=pltpu.VMEM)],
        out_specs=pl.BlockSpec(memory_space=pltpu.VMEM),
        scratch_shapes=[
            vm(NY, 2 * ROWS, YB), vm(ROWS, 2 * HALF), vm(2, NY, 128, YB), vm(ROWS, RANK),
            vm(2, 8, ROWS), vm(8, ROWS), vm(ROWS, 8),
            vm(n, 2 * ROWS, RANK), vm(n, NY, YB, RANK), vm(n, 2, 128, RANK), vm(n, 2, YB, RANK),
            vm(n, NY, 8, RANK), vm(n, NZ, 8, RANK), vm(n, NZ, ZB, RANK), vm(n, NZ, ZB, RANK),
            vm(n, NX, ZS, RANK),
            vm(n, NY, YB, RANK), vm(2 * ROWS, RANK), vm(n, 2, ROWS, RANK),
            vm(n, 32, 1, 128), vm(ROWS, RANK), vm(2, ROWS, RANK),
            pltpu.SemaphoreType.DMA, dma(2, 2, NY), dma(2, NY), dma(2, NY),
            dma(2, NY), dma(NY, 2), pltpu.SemaphoreType.DMA, pltpu.SemaphoreType.DMA,
            dma(2), dma(2), dma(n), dma(n), dma(n, 6), dma(n, 6), dma(n, 2), dma(n, 2),
            dma(n), dma(n), dma(n), dma(n), dma(n), dma(n), dma(n, 2), dma(n, 2), dma(n, 6), dma(n, 6),
            dma(n), dma(n), dma(n), dma(n), dma(n), dma(n), dma(2), dma(2),
        ],
        compiler_params=pltpu.CompilerParams(
            collective_id=0, has_side_effects=True, vmem_limit_bytes=62 << 20
        ),
        name="steps",
    )(points, log_factor, mass)
    return RANK * share


def solution(mesh):
    split = Mesh(mesh.devices.reshape(2, 2, 4, 2, 8), AXES)
    rows = ("xl", "c", "y", "xh", "z")
    return jax.shard_map(
        body,
        mesh=split,
        in_specs=(P(rows, None), P(rows, None), P(rows)),
        out_specs=P(rows, None),
        check_vma=False,
    )
```

```python
import functools

import jax
import jax.numpy as jnp
from jax import lax
from jax.experimental import pallas as pl
from jax.experimental.pallas import tpu as pltpu
from jax.sharding import Mesh
from jax.sharding import PartitionSpec as P

ITERS = 2
STEP_SCALE = 4.0
AXES = ("xl", "c", "y", "xh", "z")
NY, NZ, NX = 4, 8, 4
ROWS = 256
RANK = 256
HALF = 1024
YB = HALF // NY
ZB = YB // NZ
ZS = ZB + 8
ZA, ZY = ZB - 8, 8
YA = NZ * ZA
HIGHEST = lax.Precision.HIGHEST


def dot0(a, b):
    return lax.dot_general(
        a, b, (((0,), (0,)), ((), ())), precision=HIGHEST, preferred_element_type=jnp.float32
    )


def dot1(a, b):
    return lax.dot_general(
        a, b, (((1,), (0,)), ((), ())), precision=HIGHEST, preferred_element_type=jnp.float32
    )


def kernel(
    points, lf_in, mass, out,
    pts, pv, relay, lf, meta, meta_out, percol, scaled, mom, ring1, ring2, stat, statz, zsend, zrecv, xall, gath, acc, part,
    mx, grad, fin,
    r_pv, s_rel, r_rel, s_fwd, s_pts, r_pts, s_lf, r_lf, s_meta, r_meta, s_sc, r_sc, s_r, r_r, s_st, r_st,
    s_z, r_z, s_x, r_x, s_gz, r_gz, s_gb, r_gb, s_gy, r_gy, s_pt, r_pt, s_mc, r_mc, s_my, r_my,
    s_fin, r_fin,
):
    xl, c, y, xh, z = (lax.axis_index(a) for a in AXES)
    x = 2 * xh + xl
    other = 1 - c
    swp = xl * ((c + xh) % 2)
    vc = (c + swp) % 2
    vxh = (xh + swp) % 2
    swapped = swp == 1

    def at(c_=None, x_=None, y_=None, z_=None):
        x_ = x if x_ is None else x_
        return (
            x_ % 2,
            c if c_ is None else c_,
            y if y_ is None else y_,
            x_ // 2,
            z if z_ is None else z_,
        )

    xq = 2 * vxh + xl
    yo = [(y + j) % NY for j in range(NY)]
    zo = [(z + j) % NZ for j in range(NZ)]
    xo = [(x + j) % NX for j in range(NX)]

    def hops(k, n):
        return min(k, n - k)

    zf = sorted(range(1, NZ), key=lambda j: -hops(j, NZ))
    xf = sorted(range(1, NX), key=lambda j: -hops(j, NX))
    cz = [(i, j) for i in range(2) for j in range(NZ)]
    cz = sorted(cz, key=lambda k: -hops(k[1], NZ) - 0.5 * k[0])
    cz = [(c if i == 0 else other, zo[j]) for i, j in cz]
    xy = [(i, j) for i in range(NX) for j in range(NY)]
    xy = sorted(xy, key=lambda k: -hops(k[0], NX) - hops(k[1], NY))
    xy = [(xo[i], yo[j]) for i, j in xy]
    own = pl.ds(pl.multiple_of(c * ROWS, ROWS), ROWS)
    oth = pl.ds(pl.multiple_of(other * ROWS, ROWS), ROWS)
    relays = x % 2 == 0

    def rdma(src, dst, ss, rs, dev):
        return pltpu.make_async_remote_copy(
            src_ref=src, dst_ref=dst, send_sem=ss, recv_sem=rs, device_id=dev,
            device_id_type=pl.DeviceIdType.MESH,
        )

    def sent(ref, sem):
        rdma(ref, ref, sem, sem, at(c_=other)).wait_send()

    def arrived(ref, sem):
        rdma(ref, ref, sem, sem, at(c_=other)).wait_recv()

    load = pltpu.make_async_copy(points, pv, r_pv)
    load.start()
    lf_remote = rdma(lf_in, lf, s_lf, r_lf, at(c_=vc, x_=xq))
    lf_local = pltpu.make_async_copy(lf_in, lf, r_lf)
    order = [yo[2], yo[1], yo[3], yo[0]]

    def cols(h, b, r, n):
        return points.at[pl.ds(r, n), pl.ds(pl.multiple_of(h * HALF + b * YB, YB), YB)]

    def half_local(b):
        return pltpu.make_async_copy(cols(c, b, 0, ROWS), pts.at[b, own], r_pts.at[b, c])

    def half_out(b):
        return rdma(cols(other, b, 0, ROWS), pts.at[b, own], s_pts.at[0, b], r_pts.at[b, c],
                    at(c_=other))

    def piece(j, h, r):
        return rdma(cols(h, order[j], r * 128, 128), relay.at[r, j], s_rel.at[h, r, j],
                    r_rel.at[r, j], at(c_=h, x_=xo[1] if r == 0 else xo[3]))

    def forward(j, r):
        to = xo[1] if r == 0 else xo[3]
        slot = (3 - to) // 2
        rows = pl.ds(pl.multiple_of(slot * ROWS + r * 128, 128), 128)
        return rdma(relay.at[r, j], pts.at[order[j], rows], s_fwd.at[r, j],
                    r_pts.at[order[j], slot], at(x_=to))

    @pl.when(jnp.logical_not(swapped))
    def _():
        lf_local.start()
        for b in order:
            half_local(b).start()

    barrier = pltpu.get_barrier_semaphore()
    peers = [at(c_=a, z_=b) for a, b in cz[:-1]] + [at(x_=a, y_=b) for a, b in xy[:-1]]
    peers += [at(c_=other, x_=b) for b in xo[1:]]
    for p in peers:
        pl.semaphore_signal(barrier, inc=1, device_id=p, device_id_type=pl.DeviceIdType.MESH)

    load.wait()
    squares = jnp.zeros((ROWS, 1), jnp.float32)
    for k in range(8):
        part_k = pv[:, k * 256 : (k + 1) * 256]
        squares += jnp.sum(part_k * part_k, axis=1, keepdims=True)
    squares_row = jnp.transpose(jnp.broadcast_to(squares, (ROWS, 128)))[:8]
    row = lax.broadcasted_iota(jnp.int32, (8, ROWS), 0)
    meta_out[...] = jnp.where(
        row == 0, squares_row, jnp.where(row == 1, 1.0, jnp.where(row == 2, mass[...], 0.0))
    )
    pl.semaphore_wait(barrier, len(peers))

    meta_remote = rdma(meta_out, meta.at[vc], s_meta.at[0], r_meta.at[vc],
                       at(c_=other, x_=xq))
    meta_own = rdma(meta_out, meta.at[vc], s_meta.at[1], r_meta.at[vc], at(c_=c, x_=xq))
    meta_local = pltpu.make_async_copy(meta_out, meta.at[vc], r_meta.at[vc])
    meta_remote.start()

    @pl.when(swapped)
    def _():
        meta_own.start()

    @pl.when(jnp.logical_not(swapped))
    def _():
        meta_local.start()

    def each_piece(j, act):
        for r in range(2):
            for h in range(2):
                act(piece(j, h, r))

    def start(cpy):
        cpy.start()

    def wait_send(cpy):
        cpy.wait_send()

    @pl.when(swapped)
    def _():
        lf_remote.start()
        each_piece(0, start)
        lf_remote.wait_send()
        each_piece(1, start)

    @pl.when(jnp.logical_not(swapped))
    def _():
        for b in order:
            half_out(b).start()

    lf_remote.wait_recv()
    for v in range(2):
        rdma(meta_out, meta.at[v], s_meta.at[0], r_meta.at[v], at(c_=other)).wait_recv()
    percol[...] = jnp.transpose(meta[c])

    def wait_points(b):
        for v in range(2):
            dst = pts.at[b, pl.ds(v * ROWS, ROWS)]
            rdma(dst, dst, s_pts.at[0, b], r_pts.at[b, v], at(c_=other)).wait_recv()

    def step(it, _):
        for k in range(2):
            half = slice(k * 128, (k + 1) * 128)
            v = lf[half]
            e = jnp.exp(v - jnp.max(v, axis=1, keepdims=True))
            rows = pl.ds(pl.multiple_of(c * ROWS + k * 128, 128), 128)
            scaled[it, rows] = e / jnp.sum(e, axis=1, keepdims=True) * percol[half, 2:3]
            rdma(scaled.at[it, rows], scaled.at[it, rows], s_sc.at[it], r_sc.at[it],
                 at(c_=other)).start()
        last = it == ITERS - 1

        @pl.when(last)
        def _():
            @pl.when(swapped)
            def _():
                rdma(lf, fin.at[0], s_fin.at[0], r_fin.at[0], at(c_=vc, x_=xq)).start()

        def pass_on(j):
            @pl.when((it == 0) & relays)
            def _():
                for r in range(2):
                    piece(j, c, r).wait_recv()
                    forward(j, r).start()

        def ready(j):
            if j < 3:
                pass_on(j)

            @pl.when(it == 0)
            def _():
                if j < 2:
                    @pl.when(swapped)
                    def _():
                        each_piece(j, wait_send)
                        each_piece(j + 2, start)

                wait_points(order[j])

        def moment(j):
            ready(j)
            return dot0(pts[order[j]], scaled[it])

        lo, hi = pl.ds(0, 128), pl.ds(128, 128)
        up, dn = at(y_=yo[1]), at(y_=yo[3])
        ready(0)
        mom[it, 2] = dot0(pts[order[0], own], scaled[it, own])
        arrived(scaled.at[it, oth], r_sc.at[it])
        mom[it, 2] += dot0(pts[order[0], oth], scaled[it, oth])

        def ring(k, rows, dst, n, dev):
            cpy = rdma(mom.at[it, k, rows], dst, s_r.at[it, n], r_r.at[it, n], dev)
            cpy.start()
            return cpy

        up1 = ring(2, lo, ring1.at[it, 0], 0, up)
        dn1 = ring(2, hi, ring1.at[it, 1], 1, dn)
        mom[it, 1] = moment(1)
        up2 = ring(1, hi, ring2.at[it, 0, hi], 2, up)
        mom[it, 3] = moment(2)
        dn2 = ring(3, lo, ring2.at[it, 1, lo], 3, dn)
        pass_on(3)
        stat[it, 0] = dot1(meta[0], scaled[it, :ROWS]) + dot1(meta[1], scaled[it, ROWS:])
        for j in range(1, NY):
            rdma(stat.at[it, 0], stat.at[it, j], s_st.at[it, 0], r_st.at[it, 0],
                 at(y_=yo[j])).start()
        up1.wait_recv()
        mom[it, 1, lo] += ring1[it, 0]
        up3 = ring(1, lo, ring2.at[it, 0, lo], 4, up)
        dn1.wait_recv()
        mom[it, 3, hi] += ring1[it, 1]
        dn3 = ring(3, hi, ring2.at[it, 1, hi], 5, dn)

        mom[it, 0] = moment(3)

        arrived(stat.at[it, pl.ds(1, NY - 1)], r_st.at[it, 0])
        statz[it, 0] = stat[it, 0] + stat[it, 1] + stat[it, 2] + stat[it, 3]
        for j in zf:
            rdma(statz.at[it, 0], statz.at[it, j], s_st.at[it, 1], r_st.at[it, 1],
                 at(z_=zo[j])).start()
        for cpy in (up2, dn2, up3, dn3):
            cpy.wait_recv()

        def fill(k):
            for dst, n, first in ((0, ZA, k * ZA), (ZA, ZY, YA + k * ZY)):
                r = pl.ds(pl.multiple_of(first, 8), n)
                zsend[it, k, dst : dst + n] = mom[it, 0, r] + ring2[it, 0, r] + ring2[it, 1, r]

        for j in zf:
            fill(zo[j])
            rdma(zsend.at[it, zo[j]], zrecv.at[it, j], s_z.at[it], r_z.at[it],
                 at(z_=zo[j])).start()
        fill(z)
        arrived(zrecv.at[it, pl.ds(1, NZ - 1)], r_z.at[it])
        shard = zsend[it, z]
        for j in range(1, NZ):
            shard += zrecv[it, j]
        arrived(statz.at[it, pl.ds(1, NZ - 1)], r_st.at[it, 1])

        xall[it, x, :ZB] = shard
        xall[it, x, ZB:] = jnp.sum(statz[it], axis=0)
        for j in xf:
            rdma(xall.at[it, x], xall.at[it, x], s_x.at[it], r_x.at[it], at(x_=xo[j])).start()
        arrived(xall.at[it, pl.ds(0, NX - 1)], r_x.at[it])
        source = xall[it, 0] + xall[it, 1] + xall[it, 2]
        target = xall[it, 3]
        is_target = x == 3
        facing = jnp.where(is_target, source, target)

        zrows = pl.ds(pl.multiple_of(z * ZA, 8), ZA)
        yrows = pl.ds(pl.multiple_of(YA + z * ZY, 8), ZY)
        gath[it, y, zrows] = facing[:ZA]
        gath[it, y, yrows] = facing[ZA:ZB]
        for j in (2, 1, 3):
            rdma(gath.at[it, y, yrows], gath.at[it, y, yrows], s_gb.at[it, 0], r_gb.at[it, 0],
                 at(y_=yo[j])).start()
        for j in zf:
            rdma(gath.at[it, y, zrows], gath.at[it, y, zrows], s_gz.at[it], r_gz.at[it],
                 at(z_=zo[j])).start()
        source_mass = jnp.sum(source[ZB + 1 : ZB + 2])
        target_mass = jnp.sum(target[ZB + 1 : ZB + 2])
        facing_mass = jnp.where(is_target, source_mass, target_mass)
        marginal = 0.5 * (source[ZB + 1 : ZB + 2] / source_mass
                          + target[ZB + 1 : ZB + 2] / target_mass)
        arrived(gath.at[it, pl.ds(0, NY - 1), yrows], r_gb.at[it, 0])
        every = gath.at[it, pl.ds(0, NY), yrows]
        for j in zf:
            rdma(every, every, s_gb.at[it, 1], r_gb.at[it, 1], at(z_=zo[j])).start()
        arrived(gath.at[it, y, pl.ds(0, (NZ - 1) * ZA)], r_gz.at[it])
        glo, ghi = pl.ds(0, YA // 2), pl.ds(YA // 2, YA // 2)

        def block(b, rows, n, dev):
            ref = gath.at[it, b, rows]
            return rdma(ref, ref, s_gy.at[it, n], r_gy.at[it, n], dev)

        gout = [block(y, glo, 0, up), block(y, ghi, 1, dn), block(y, ghi, 2, up),
                block(y, glo, 3, dn)]
        for cpy in gout:
            cpy.start()
        block(yo[3], glo, 0, up).wait_recv()
        gout += [block(yo[3], glo, 4, up)]
        gout[4].start()
        block(yo[1], ghi, 1, dn).wait_recv()
        gout += [block(yo[1], ghi, 5, dn)]
        gout[5].start()
        arrived(gath.at[it, 0, pl.ds(0, (NZ - 1) * NY * ZY)], r_gb.at[it, 1])
        acc[...] = dot1(pts[y], gath[it, y])
        block(yo[3], ghi, 2, up).wait_recv()
        acc[...] += dot1(pts[yo[3]], gath[it, yo[3]])
        block(yo[1], glo, 3, dn).wait_recv()
        acc[...] += dot1(pts[yo[1]], gath[it, yo[1]])
        block(yo[2], glo, 4, up).wait_recv()
        block(yo[2], ghi, 5, dn).wait_recv()
        part[it, 0] = acc[oth] + dot1(pts[yo[2], oth], gath[it, yo[2]])
        pc = rdma(part.at[it, 0], part.at[it, 1], s_pt.at[it], r_pt.at[it], at(c_=other))
        pc.start()
        cross = acc[own] + dot1(pts[yo[2], own], gath[it, yo[2]])
        pc.wait_recv()
        cross += part[it, 1]

        facing_columns = facing[ZB + 1 : ZB + 2]
        facing_norms = facing[ZB : ZB + 1]
        squares_own = percol[:, 0:1]
        g = (
            squares_own * (facing_columns / facing_mass)
            + cross * (-2.0 / facing_mass)
            + facing_norms / facing_mass
        ) * (1.0 / marginal)
        grad[...] = g
        centred = g - jnp.sum(g, axis=1, keepdims=True) * (1.0 / RANK)
        largest = jnp.max(jnp.abs(centred))

        @pl.when(last)
        def _():
            @pl.when(swapped)
            def _():
                rdma(grad, fin.at[1], s_fin.at[1], r_fin.at[1], at(c_=vc, x_=xq)).start()

        tile = (1, 128)
        mx[it, 0] = jnp.full(tile, largest)
        for j in range(1, 16):
            rdma(mx.at[it, 0], mx.at[it, j], s_mc.at[it], r_mc.at[it],
                 at(c_=cz[j - 1][0], z_=cz[j - 1][1])).start()
        for cpy in [up1, dn1, up2, dn2, up3, dn3, pc] + gout:
            cpy.wait_send()
        sent(scaled.at[it, own], s_sc.at[it])
        sent(stat.at[it, pl.ds(1, NY - 1)], s_st.at[it, 0])
        sent(statz.at[it, pl.ds(1, NZ - 1)], s_st.at[it, 1])
        sent(zrecv.at[it, pl.ds(1, NZ - 1)], s_z.at[it])
        sent(xall.at[it, pl.ds(0, NX - 1)], s_x.at[it])
        sent(gath.at[it, y, pl.ds(0, (NZ - 1) * ZA)], s_gz.at[it])
        sent(gath.at[it, pl.ds(0, NY - 1), yrows], s_gb.at[it, 0])
        sent(gath.at[it, 0, pl.ds(0, (NZ - 1) * NY * ZY)], s_gb.at[it, 1])
        arrived(mx.at[it, pl.ds(1, 15)], r_mc.at[it])
        mx[it, 16] = jnp.max(mx[it, :16], axis=0)
        for j in range(1, 16):
            rdma(mx.at[it, 16], mx.at[it, 16 + j], s_my.at[it], r_my.at[it],
                 at(x_=xy[j - 1][0], y_=xy[j - 1][1])).start()
        sent(mx.at[it, pl.ds(1, 15)], s_mc.at[it])
        arrived(mx.at[it, pl.ds(17, 15)], r_my.at[it])
        m = jnp.max(mx[it, 16:32], axis=0)
        rate = STEP_SCALE / (m[0:1, 0:1] + 1e-6)

        @pl.when(jnp.logical_not(last))
        def _():
            lf[...] = lf[...] - rate * grad[...]

        @pl.when(last)
        def _():
            def finish(a, b):
                u = a - rate * b
                ex = jnp.exp(u - jnp.max(u, axis=1, keepdims=True))
                out[...] = ex / jnp.sum(ex, axis=1, keepdims=True)

            @pl.when(swapped)
            def _():
                for k, src in ((0, lf), (1, grad)):
                    cpy = rdma(src, fin.at[k], s_fin.at[k], r_fin.at[k], at(c_=vc, x_=xq))
                    cpy.wait_send()
                    cpy.wait_recv()
                finish(fin[0], fin[1])

            @pl.when(jnp.logical_not(swapped))
            def _():
                finish(lf[...], grad[...])

        sent(mx.at[it, pl.ds(17, 15)], s_my.at[it])
        return 0

    lax.fori_loop(0, ITERS, step, 0)

    meta_remote.wait_send()

    @pl.when(swapped)
    def _():
        meta_own.wait_send()
        for j in range(2, NY):
            each_piece(j, wait_send)

    @pl.when(jnp.logical_not(swapped))
    def _():
        for b in order:
            half_out(b).wait_send()

    @pl.when(relays)
    def _():
        for j in range(NY):
            for r in range(2):
                forward(j, r).wait_send()


def body(points, log_factor, masses):
    mass = masses.reshape(1, ROWS)
    f32 = jnp.float32
    vm = lambda *s: pltpu.VMEM(s, f32)
    dma = lambda *s: pltpu.SemaphoreType.DMA(s)
    n = ITERS
    share = pl.pallas_call(
        kernel,
        out_shape=pltpu.VMEM((ROWS, RANK), f32),
        in_specs=[pl.BlockSpec(memory_space=pltpu.HBM)] * 2
        + [pl.BlockSpec(memory_space=pltpu.VMEM)],
        out_specs=pl.BlockSpec(memory_space=pltpu.VMEM),
        scratch_shapes=[
            vm(NY, 2 * ROWS, YB), vm(ROWS, 2 * HALF), vm(2, NY, 128, YB), vm(ROWS, RANK),
            vm(2, 8, ROWS), vm(8, ROWS), vm(ROWS, 8),
            vm(n, 2 * ROWS, RANK), vm(n, NY, YB, RANK), vm(n, 2, 128, RANK), vm(n, 2, YB, RANK),
            vm(n, NY, 8, RANK), vm(n, NZ, 8, RANK), vm(n, NZ, ZB, RANK), vm(n, NZ, ZB, RANK),
            vm(n, NX, ZS, RANK),
            vm(n, NY, YB, RANK), vm(2 * ROWS, RANK), vm(n, 2, ROWS, RANK),
            vm(n, 32, 1, 128), vm(ROWS, RANK), vm(2, ROWS, RANK),
            pltpu.SemaphoreType.DMA, dma(2, 2, NY), dma(2, NY), dma(2, NY),
            dma(2, NY), dma(NY, 2), pltpu.SemaphoreType.DMA, pltpu.SemaphoreType.DMA,
            dma(2), dma(2), dma(n), dma(n), dma(n, 6), dma(n, 6), dma(n, 2), dma(n, 2),
            dma(n), dma(n), dma(n), dma(n), dma(n), dma(n), dma(n, 2), dma(n, 2), dma(n, 6), dma(n, 6),
            dma(n), dma(n), dma(n), dma(n), dma(n), dma(n), dma(2), dma(2),
        ],
        compiler_params=pltpu.CompilerParams(
            collective_id=0, has_side_effects=True, vmem_limit_bytes=62 << 20
        ),
        name="steps",
    )(points, log_factor, mass)
    return RANK * share


def solution(mesh):
    split = Mesh(mesh.devices.reshape(2, 2, 4, 2, 8), AXES)
    rows = ("xl", "c", "y", "xh", "z")
    return jax.shard_map(
        body,
        mesh=split,
        in_specs=(P(rows, None), P(rows, None), P(rows)),
        out_specs=P(rows, None),
        check_vma=False,
    )
```

```python
import functools

import jax
import jax.numpy as jnp
from jax import lax
from jax.experimental import pallas as pl
from jax.experimental.pallas import tpu as pltpu
from jax.sharding import Mesh
from jax.sharding import PartitionSpec as P

ITERS = 2
STEP_SCALE = 4.0
AXES = ("xl", "c", "y", "xh", "z")
NY, NZ, NX = 4, 8, 4
ROWS = 256
RANK = 256
HALF = 1024
YB = HALF // NY
ZB = YB // NZ
ZS = ZB + 8
ZA, ZY = ZB - 8, 8
YA = NZ * ZA
HIGHEST = lax.Precision.HIGHEST


def dot0(a, b):
    return lax.dot_general(
        a, b, (((0,), (0,)), ((), ())), precision=HIGHEST, preferred_element_type=jnp.float32
    )


def dot1(a, b):
    return lax.dot_general(
        a, b, (((1,), (0,)), ((), ())), precision=HIGHEST, preferred_element_type=jnp.float32
    )


def kernel(
    points, lf_in, mass, out,
    pts, pv, relay, lf, meta, meta_out, percol, scaled, mom, ring1, ring2, stat, statz, zsend, zrecv, xall, gath, acc, part,
    mx, grad, fin,
    r_pv, s_rel, r_rel, s_fwd, s_pts, r_pts, s_lf, r_lf, s_meta, r_meta, s_sc, r_sc, s_r, r_r, s_st, r_st,
    s_z, r_z, s_x, r_x, s_gz, r_gz, s_gb, r_gb, s_gy, r_gy, s_pt, r_pt, s_mc, r_mc, s_my, r_my,
    s_fin, r_fin,
):
    xl, c, y, xh, z = (lax.axis_index(a) for a in AXES)
    x = 2 * xh + xl
    other = 1 - c
    swp = xl * ((c + xh) % 2)
    vc = (c + swp) % 2
    vxh = (xh + swp) % 2
    swapped = swp == 1

    def at(c_=None, x_=None, y_=None, z_=None):
        x_ = x if x_ is None else x_
        return (
            x_ % 2,
            c if c_ is None else c_,
            y if y_ is None else y_,
            x_ // 2,
            z if z_ is None else z_,
        )

    xq = 2 * vxh + xl
    yo = [(y + j) % NY for j in range(NY)]
    zo = [(z + j) % NZ for j in range(NZ)]
    xo = [(x + j) % NX for j in range(NX)]

    def hops(k, n):
        return min(k, n - k)

    zf = sorted(range(1, NZ), key=lambda j: -hops(j, NZ))
    xf = sorted(range(1, NX), key=lambda j: -hops(j, NX))
    cz = [(i, j) for i in range(2) for j in range(NZ)]
    cz = sorted(cz, key=lambda k: -hops(k[1], NZ) - 0.5 * k[0])
    cz = [(c if i == 0 else other, zo[j]) for i, j in cz]
    xy = [(i, j) for i in range(NX) for j in range(NY)]
    xy = sorted(xy, key=lambda k: -hops(k[0], NX) - hops(k[1], NY))
    xy = [(xo[i], yo[j]) for i, j in xy]
    own = pl.ds(pl.multiple_of(c * ROWS, ROWS), ROWS)
    oth = pl.ds(pl.multiple_of(other * ROWS, ROWS), ROWS)
    relays = x % 2 == 0

    def rdma(src, dst, ss, rs, dev):
        return pltpu.make_async_remote_copy(
            src_ref=src, dst_ref=dst, send_sem=ss, recv_sem=rs, device_id=dev,
            device_id_type=pl.DeviceIdType.MESH,
        )

    def sent(ref, sem):
        rdma(ref, ref, sem, sem, at(c_=other)).wait_send()

    def arrived(ref, sem):
        rdma(ref, ref, sem, sem, at(c_=other)).wait_recv()

    load = pltpu.make_async_copy(points, pv, r_pv)
    load.start()
    lf_remote = rdma(lf_in, lf, s_lf, r_lf, at(c_=vc, x_=xq))
    lf_local = pltpu.make_async_copy(lf_in, lf, r_lf)
    order = [yo[2], yo[1], yo[3], yo[0]]

    def cols(h, b, r, n):
        return points.at[pl.ds(r, n), pl.ds(pl.multiple_of(h * HALF + b * YB, YB), YB)]

    def half_local(b):
        return pltpu.make_async_copy(cols(c, b, 0, ROWS), pts.at[b, own], r_pts.at[b, c])

    def half_out(b):
        return rdma(cols(other, b, 0, ROWS), pts.at[b, own], s_pts.at[0, b], r_pts.at[b, c],
                    at(c_=other))

    def piece(j, h, r):
        return rdma(cols(h, order[j], r * 128, 128), relay.at[r, j], s_rel.at[h, r, j],
                    r_rel.at[r, j], at(c_=h, x_=xo[1] if r == 0 else xo[3]))

    def forward(j, r):
        to = xo[1] if r == 0 else xo[3]
        slot = (3 - to) // 2
        rows = pl.ds(pl.multiple_of(slot * ROWS + r * 128, 128), 128)
        return rdma(relay.at[r, j], pts.at[order[j], rows], s_fwd.at[r, j],
                    r_pts.at[order[j], slot], at(x_=to))

    @pl.when(jnp.logical_not(swapped))
    def _():
        lf_local.start()
        for b in order:
            half_local(b).start()

    barrier = pltpu.get_barrier_semaphore()
    peers = [at(c_=a, z_=b) for a, b in cz[:-1]] + [at(x_=a, y_=b) for a, b in xy[:-1]]
    peers += [at(c_=other, x_=b) for b in xo[1:]]
    for p in peers:
        pl.semaphore_signal(barrier, inc=1, device_id=p, device_id_type=pl.DeviceIdType.MESH)

    load.wait()
    squares = jnp.zeros((ROWS, 1), jnp.float32)
    for k in range(8):
        part_k = pv[:, k * 256 : (k + 1) * 256]
        squares += jnp.sum(part_k * part_k, axis=1, keepdims=True)
    squares_row = jnp.transpose(jnp.broadcast_to(squares, (ROWS, 128)))[:8]
    row = lax.broadcasted_iota(jnp.int32, (8, ROWS), 0)
    meta_out[...] = jnp.where(
        row == 0, squares_row, jnp.where(row == 1, 1.0, jnp.where(row == 2, mass[...], 0.0))
    )
    pl.semaphore_wait(barrier, len(peers))

    meta_remote = rdma(meta_out, meta.at[vc], s_meta.at[0], r_meta.at[vc],
                       at(c_=other, x_=xq))
    meta_own = rdma(meta_out, meta.at[vc], s_meta.at[1], r_meta.at[vc], at(c_=c, x_=xq))
    meta_local = pltpu.make_async_copy(meta_out, meta.at[vc], r_meta.at[vc])
    meta_remote.start()

    @pl.when(swapped)
    def _():
        meta_own.start()

    @pl.when(jnp.logical_not(swapped))
    def _():
        meta_local.start()

    def each_piece(j, act):
        for r in range(2):
            for h in range(2):
                act(piece(j, h, r))

    def start(cpy):
        cpy.start()

    def wait_send(cpy):
        cpy.wait_send()

    @pl.when(swapped)
    def _():
        lf_remote.start()
        each_piece(0, start)
        lf_remote.wait_send()
        each_piece(1, start)
        each_piece(2, start)

    @pl.when(jnp.logical_not(swapped))
    def _():
        for b in order:
            half_out(b).start()

    lf_remote.wait_recv()
    for v in range(2):
        rdma(meta_out, meta.at[v], s_meta.at[0], r_meta.at[v], at(c_=other)).wait_recv()
    percol[...] = jnp.transpose(meta[c])

    def wait_points(b):
        for v in range(2):
            dst = pts.at[b, pl.ds(v * ROWS, ROWS)]
            rdma(dst, dst, s_pts.at[0, b], r_pts.at[b, v], at(c_=other)).wait_recv()

    def step(it, _):
        for k in range(2):
            half = slice(k * 128, (k + 1) * 128)
            v = lf[half]
            e = jnp.exp(v - jnp.max(v, axis=1, keepdims=True))
            rows = pl.ds(pl.multiple_of(c * ROWS + k * 128, 128), 128)
            scaled[it, rows] = e / jnp.sum(e, axis=1, keepdims=True) * percol[half, 2:3]
            rdma(scaled.at[it, rows], scaled.at[it, rows], s_sc.at[it], r_sc.at[it],
                 at(c_=other)).start()
        last = it == ITERS - 1

        @pl.when(last)
        def _():
            @pl.when(swapped)
            def _():
                rdma(lf, fin.at[0], s_fin.at[0], r_fin.at[0], at(c_=vc, x_=xq)).start()

        def pass_on(j):
            @pl.when((it == 0) & relays)
            def _():
                for r in range(2):
                    piece(j, c, r).wait_recv()
                    forward(j, r).start()

        def ready(j):
            if j < 3:
                pass_on(j)

            @pl.when(it == 0)
            def _():
                if j == 0:
                    @pl.when(swapped)
                    def _():
                        each_piece(j, wait_send)
                        each_piece(j + 3, start)

                wait_points(order[j])

        def moment(j):
            ready(j)
            return dot0(pts[order[j]], scaled[it])

        lo, hi = pl.ds(0, 128), pl.ds(128, 128)
        up, dn = at(y_=yo[1]), at(y_=yo[3])
        ready(0)
        mom[it, 2] = dot0(pts[order[0], own], scaled[it, own])
        arrived(scaled.at[it, oth], r_sc.at[it])
        mom[it, 2] += dot0(pts[order[0], oth], scaled[it, oth])

        def ring(k, rows, dst, n, dev):
            cpy = rdma(mom.at[it, k, rows], dst, s_r.at[it, n], r_r.at[it, n], dev)
            cpy.start()
            return cpy

        up1 = ring(2, lo, ring1.at[it, 0], 0, up)
        dn1 = ring(2, hi, ring1.at[it, 1], 1, dn)
        mom[it, 1] = moment(1)
        up2 = ring(1, hi, ring2.at[it, 0, hi], 2, up)
        mom[it, 3] = moment(2)
        dn2 = ring(3, lo, ring2.at[it, 1, lo], 3, dn)
        pass_on(3)
        stat[it, 0] = dot1(meta[0], scaled[it, :ROWS]) + dot1(meta[1], scaled[it, ROWS:])
        for j in range(1, NY):
            rdma(stat.at[it, 0], stat.at[it, j], s_st.at[it, 0], r_st.at[it, 0],
                 at(y_=yo[j])).start()
        up1.wait_recv()
        mom[it, 1, lo] += ring1[it, 0]
        up3 = ring(1, lo, ring2.at[it, 0, lo], 4, up)
        dn1.wait_recv()
        mom[it, 3, hi] += ring1[it, 1]
        dn3 = ring(3, hi, ring2.at[it, 1, hi], 5, dn)

        mom[it, 0] = moment(3)

        arrived(stat.at[it, pl.ds(1, NY - 1)], r_st.at[it, 0])
        statz[it, 0] = stat[it, 0] + stat[it, 1] + stat[it, 2] + stat[it, 3]
        for j in zf:
            rdma(statz.at[it, 0], statz.at[it, j], s_st.at[it, 1], r_st.at[it, 1],
                 at(z_=zo[j])).start()
        for cpy in (up2, dn2, up3, dn3):
            cpy.wait_recv()

        def fill(k):
            for dst, n, first in ((0, ZA, k * ZA), (ZA, ZY, YA + k * ZY)):
                r = pl.ds(pl.multiple_of(first, 8), n)
                zsend[it, k, dst : dst + n] = mom[it, 0, r] + ring2[it, 0, r] + ring2[it, 1, r]

        for j in zf:
            fill(zo[j])
            rdma(zsend.at[it, zo[j]], zrecv.at[it, j], s_z.at[it], r_z.at[it],
                 at(z_=zo[j])).start()
        fill(z)
        arrived(zrecv.at[it, pl.ds(1, NZ - 1)], r_z.at[it])
        shard = zsend[it, z]
        for j in range(1, NZ):
            shard += zrecv[it, j]
        arrived(statz.at[it, pl.ds(1, NZ - 1)], r_st.at[it, 1])

        xall[it, x, :ZB] = shard
        xall[it, x, ZB:] = jnp.sum(statz[it], axis=0)
        for j in xf:
            rdma(xall.at[it, x], xall.at[it, x], s_x.at[it], r_x.at[it], at(x_=xo[j])).start()
        arrived(xall.at[it, pl.ds(0, NX - 1)], r_x.at[it])
        source = xall[it, 0] + xall[it, 1] + xall[it, 2]
        target = xall[it, 3]
        is_target = x == 3
        facing = jnp.where(is_target, source, target)

        zrows = pl.ds(pl.multiple_of(z * ZA, 8), ZA)
        yrows = pl.ds(pl.multiple_of(YA + z * ZY, 8), ZY)
        gath[it, y, zrows] = facing[:ZA]
        gath[it, y, yrows] = facing[ZA:ZB]
        for j in (2, 1, 3):
            rdma(gath.at[it, y, yrows], gath.at[it, y, yrows], s_gb.at[it, 0], r_gb.at[it, 0],
                 at(y_=yo[j])).start()
        for j in zf:
            rdma(gath.at[it, y, zrows], gath.at[it, y, zrows], s_gz.at[it], r_gz.at[it],
                 at(z_=zo[j])).start()
        source_mass = jnp.sum(source[ZB + 1 : ZB + 2])
        target_mass = jnp.sum(target[ZB + 1 : ZB + 2])
        facing_mass = jnp.where(is_target, source_mass, target_mass)
        marginal = 0.5 * (source[ZB + 1 : ZB + 2] / source_mass
                          + target[ZB + 1 : ZB + 2] / target_mass)
        arrived(gath.at[it, pl.ds(0, NY - 1), yrows], r_gb.at[it, 0])
        every = gath.at[it, pl.ds(0, NY), yrows]
        for j in zf:
            rdma(every, every, s_gb.at[it, 1], r_gb.at[it, 1], at(z_=zo[j])).start()
        arrived(gath.at[it, y, pl.ds(0, (NZ - 1) * ZA)], r_gz.at[it])
        glo, ghi = pl.ds(0, YA // 2), pl.ds(YA // 2, YA // 2)

        def block(b, rows, n, dev):
            ref = gath.at[it, b, rows]
            return rdma(ref, ref, s_gy.at[it, n], r_gy.at[it, n], dev)

        gout = [block(y, glo, 0, up), block(y, ghi, 1, dn), block(y, ghi, 2, up),
                block(y, glo, 3, dn)]
        for cpy in gout:
            cpy.start()
        block(yo[3], glo, 0, up).wait_recv()
        gout += [block(yo[3], glo, 4, up)]
        gout[4].start()
        block(yo[1], ghi, 1, dn).wait_recv()
        gout += [block(yo[1], ghi, 5, dn)]
        gout[5].start()
        arrived(gath.at[it, 0, pl.ds(0, (NZ - 1) * NY * ZY)], r_gb.at[it, 1])
        acc[...] = dot1(pts[y], gath[it, y])
        block(yo[3], ghi, 2, up).wait_recv()
        acc[...] += dot1(pts[yo[3]], gath[it, yo[3]])
        block(yo[1], glo, 3, dn).wait_recv()
        acc[...] += dot1(pts[yo[1]], gath[it, yo[1]])
        block(yo[2], glo, 4, up).wait_recv()
        block(yo[2], ghi, 5, dn).wait_recv()
        part[it, 0] = acc[oth] + dot1(pts[yo[2], oth], gath[it, yo[2]])
        pc = rdma(part.at[it, 0], part.at[it, 1], s_pt.at[it], r_pt.at[it], at(c_=other))
        pc.start()
        cross = acc[own] + dot1(pts[yo[2], own], gath[it, yo[2]])
        pc.wait_recv()
        cross += part[it, 1]

        facing_columns = facing[ZB + 1 : ZB + 2]
        facing_norms = facing[ZB : ZB + 1]
        squares_own = percol[:, 0:1]
        g = (
            squares_own * (facing_columns / facing_mass)
            + cross * (-2.0 / facing_mass)
            + facing_norms / facing_mass
        ) * (1.0 / marginal)
        grad[...] = g
        centred = g - jnp.sum(g, axis=1, keepdims=True) * (1.0 / RANK)
        largest = jnp.max(jnp.abs(centred))

        @pl.when(last)
        def _():
            @pl.when(swapped)
            def _():
                rdma(grad, fin.at[1], s_fin.at[1], r_fin.at[1], at(c_=vc, x_=xq)).start()

        tile = (1, 128)
        mx[it, 0] = jnp.full(tile, largest)
        for j in range(1, 16):
            rdma(mx.at[it, 0], mx.at[it, j], s_mc.at[it], r_mc.at[it],
                 at(c_=cz[j - 1][0], z_=cz[j - 1][1])).start()
        for cpy in [up1, dn1, up2, dn2, up3, dn3, pc] + gout:
            cpy.wait_send()
        sent(scaled.at[it, own], s_sc.at[it])
        sent(stat.at[it, pl.ds(1, NY - 1)], s_st.at[it, 0])
        sent(statz.at[it, pl.ds(1, NZ - 1)], s_st.at[it, 1])
        sent(zrecv.at[it, pl.ds(1, NZ - 1)], s_z.at[it])
        sent(xall.at[it, pl.ds(0, NX - 1)], s_x.at[it])
        sent(gath.at[it, y, pl.ds(0, (NZ - 1) * ZA)], s_gz.at[it])
        sent(gath.at[it, pl.ds(0, NY - 1), yrows], s_gb.at[it, 0])
        sent(gath.at[it, 0, pl.ds(0, (NZ - 1) * NY * ZY)], s_gb.at[it, 1])
        arrived(mx.at[it, pl.ds(1, 15)], r_mc.at[it])
        mx[it, 16] = jnp.max(mx[it, :16], axis=0)
        for j in range(1, 16):
            rdma(mx.at[it, 16], mx.at[it, 16 + j], s_my.at[it], r_my.at[it],
                 at(x_=xy[j - 1][0], y_=xy[j - 1][1])).start()
        sent(mx.at[it, pl.ds(1, 15)], s_mc.at[it])
        arrived(mx.at[it, pl.ds(17, 15)], r_my.at[it])
        m = jnp.max(mx[it, 16:32], axis=0)
        rate = STEP_SCALE / (m[0:1, 0:1] + 1e-6)

        @pl.when(jnp.logical_not(last))
        def _():
            lf[...] = lf[...] - rate * grad[...]

        @pl.when(last)
        def _():
            def finish(a, b):
                u = a - rate * b
                ex = jnp.exp(u - jnp.max(u, axis=1, keepdims=True))
                out[...] = ex / jnp.sum(ex, axis=1, keepdims=True)

            @pl.when(swapped)
            def _():
                for k, src in ((0, lf), (1, grad)):
                    cpy = rdma(src, fin.at[k], s_fin.at[k], r_fin.at[k], at(c_=vc, x_=xq))
                    cpy.wait_send()
                    cpy.wait_recv()
                finish(fin[0], fin[1])

            @pl.when(jnp.logical_not(swapped))
            def _():
                finish(lf[...], grad[...])

        sent(mx.at[it, pl.ds(17, 15)], s_my.at[it])
        return 0

    lax.fori_loop(0, ITERS, step, 0)

    meta_remote.wait_send()

    @pl.when(swapped)
    def _():
        meta_own.wait_send()
        for j in range(1, NY):
            each_piece(j, wait_send)

    @pl.when(jnp.logical_not(swapped))
    def _():
        for b in order:
            half_out(b).wait_send()

    @pl.when(relays)
    def _():
        for j in range(NY):
            for r in range(2):
                forward(j, r).wait_send()


def body(points, log_factor, masses):
    mass = masses.reshape(1, ROWS)
    f32 = jnp.float32
    vm = lambda *s: pltpu.VMEM(s, f32)
    dma = lambda *s: pltpu.SemaphoreType.DMA(s)
    n = ITERS
    share = pl.pallas_call(
        kernel,
        out_shape=pltpu.VMEM((ROWS, RANK), f32),
        in_specs=[pl.BlockSpec(memory_space=pltpu.HBM)] * 2
        + [pl.BlockSpec(memory_space=pltpu.VMEM)],
        out_specs=pl.BlockSpec(memory_space=pltpu.VMEM),
        scratch_shapes=[
            vm(NY, 2 * ROWS, YB), vm(ROWS, 2 * HALF), vm(2, NY, 128, YB), vm(ROWS, RANK),
            vm(2, 8, ROWS), vm(8, ROWS), vm(ROWS, 8),
            vm(n, 2 * ROWS, RANK), vm(n, NY, YB, RANK), vm(n, 2, 128, RANK), vm(n, 2, YB, RANK),
            vm(n, NY, 8, RANK), vm(n, NZ, 8, RANK), vm(n, NZ, ZB, RANK), vm(n, NZ, ZB, RANK),
            vm(n, NX, ZS, RANK),
            vm(n, NY, YB, RANK), vm(2 * ROWS, RANK), vm(n, 2, ROWS, RANK),
            vm(n, 32, 1, 128), vm(ROWS, RANK), vm(2, ROWS, RANK),
            pltpu.SemaphoreType.DMA, dma(2, 2, NY), dma(2, NY), dma(2, NY),
            dma(2, NY), dma(NY, 2), pltpu.SemaphoreType.DMA, pltpu.SemaphoreType.DMA,
            dma(2), dma(2), dma(n), dma(n), dma(n, 6), dma(n, 6), dma(n, 2), dma(n, 2),
            dma(n), dma(n), dma(n), dma(n), dma(n), dma(n), dma(n, 2), dma(n, 2), dma(n, 6), dma(n, 6),
            dma(n), dma(n), dma(n), dma(n), dma(n), dma(n), dma(2), dma(2),
        ],
        compiler_params=pltpu.CompilerParams(
            collective_id=0, has_side_effects=True, vmem_limit_bytes=62 << 20
        ),
        name="steps",
    )(points, log_factor, mass)
    return RANK * share


def solution(mesh):
    split = Mesh(mesh.devices.reshape(2, 2, 4, 2, 8), AXES)
    rows = ("xl", "c", "y", "xh", "z")
    return jax.shard_map(
        body,
        mesh=split,
        in_specs=(P(rows, None), P(rows, None), P(rows)),
        out_specs=P(rows, None),
        check_vma=False,
    )
```
